512 devices in a mesh: dp: 4 (over x), row: 8 (over y), col: 16 (over z, core).
Axes of the slice: x: 4, y: 8, z: 8, core: 2. Of those that a mesh axis runs over, the one named last changes fastest.
Arguments:
- tokens: bfloat16 [2048, 8192], P('dp', ('row', 'col')), may hold values from -6 to 6
- weight_codes: bfloat16 [8192, 26624], P('row', 'col'), may hold values from -0.0625 to 0.0625
- group_scales: bfloat16 [64, 26624], P('row', 'col'), may hold values from 0.25 to 4
- adapter_down: bfloat16 [8192, 64], P('row'), may hold values from -0.0625 to 0.0625
- adapter_up: bfloat16 [64, 26624], P(None, 'col'), may hold values from -0.75 to 0.75
- up_branch: bfloat16 [2048, 26624], P(('dp', 'row'), 'col'), may hold values from -6 to 6
- hidden_grad: bfloat16 [2048, 26624], P(('dp', 'row'), 'col'), may hold values from -6 to 6
Outputs:
- grad_tokens: bfloat16 [2048, 8192], P('dp', ('row', 'col'))
- grad_down: float32 [8192, 64], P('row', 'col')
- grad_up: float32 [64, 26624], P(None, 'col')
The draws below stay inside these ranges and needn't reach their ends.
All inputs are finite; a program needn't handle non-finite values.
Results may differ from the reference program's by a relative error of at most 0.034.
Values may be sent and summed in bfloat16 or wider, within the bound.
A program may use at most 64 MiB of HBM per device.

```python
import math
import jax
import jax.numpy as jnp
from jax import lax

D = 8192
FF = 26624
RANK = 64
GROUP = 128
TOKENS = 2048
N_ROW = 8
N_COL = 16


def block_levels(own_key, dims, split, least, high):
    gain, own = 1.0, jax.random.fold_in(own_key, 6)
    for dim, parts in split:
        steps = jnp.exp(jax.random.uniform(jax.random.fold_in(own, dim), (parts,), jnp.float32, least / len(split), high / len(split)))
        gain = gain * jnp.repeat(steps, dims[dim] // parts).reshape([-1 if axis == dim else 1 for axis in range(len(dims))])
    return gain


def normal_values(stream_key, dims, scale, reach, cuts=(), kind=jnp.bfloat16):
    entries = scale * jax.random.normal(stream_key, dims, jnp.float32)
    if cuts:
        entries = entries * block_levels(stream_key, dims, cuts, -0.22, 0.18)
    return jnp.clip(entries, -reach, reach).astype(kind)


def setup_inputs(seed: int = 0) -> dict:
    key_of = jax.random.split(jax.random.key(seed), 8)
    tokens = normal_values(key_of[0], (TOKENS, D), 1.0, 6.0, ((0, 4), (1, 128)))
    weight_codes = normal_values(key_of[1], (D, FF), D ** -0.5, 0.0625, ((0, 8), (1, 16)))
    group_scales = jnp.clip(jnp.exp(math.log(4.0) - 2.7725887 * jax.random.uniform(key_of[2], (D // GROUP, FF), jnp.float32) ** block_levels(key_of[2], (D // GROUP, FF), ((0, 8), (1, 16)), -0.2, 0.2)), 0.25, 4.0).astype(jnp.bfloat16)
    adapter_down = normal_values(key_of[3], (D, RANK), D ** -0.5, 0.0625, ((0, 8),))
    adapter_up = normal_values(key_of[4], (RANK, FF), RANK ** -0.5, 0.75, ((1, 16),))
    up_branch = normal_values(key_of[5], (TOKENS, FF), 1.0, 6.0, ((0, 32), (1, 16)))
    hidden_grad = normal_values(key_of[6], (TOKENS, FF), 1.0, 6.0, ((0, 32), (1, 16)))
    return dict(tokens=tokens, weight_codes=weight_codes, group_scales=group_scales, adapter_down=adapter_down, adapter_up=adapter_up, up_branch=up_branch, hidden_grad=hidden_grad)


adapter_scale = 2.0


def dequantize(weight_codes, group_scales):
    depth, width = weight_codes.shape
    grouped = weight_codes.reshape(depth // GROUP, GROUP, width).astype(jnp.float32)
    scaled = grouped * group_scales.astype(jnp.float32)[:, None, :]
    return scaled.reshape(depth, width).astype(jnp.bfloat16)


def gate_gradient(gate, hidden_grad, up_branch):
    sigma = jax.nn.sigmoid(gate)
    product = hidden_grad.astype(jnp.float32) * up_branch.astype(jnp.float32)
    return (product * sigma * (1.0 + gate * (1.0 - sigma))).astype(jnp.bfloat16)


def reference(tokens, weight_codes, group_scales, adapter_down, adapter_up, up_branch, hidden_grad):
    weight = dequantize(weight_codes, group_scales)
    count, depth = tokens.shape
    width = weight.shape[1]
    rank = adapter_down.shape[1]
    row_block = depth // N_ROW
    tok_blocks = tokens.reshape(count, N_ROW, row_block).transpose(1, 0, 2)
    weight_blocks = weight.reshape(N_ROW, row_block, width)
    down_blocks = adapter_down.reshape(N_ROW, row_block, rank)

    def row_step(carry, pieces):
        tok_piece, weight_piece, down_piece = pieces
        gate_piece = jnp.dot(tok_piece, weight_piece, preferred_element_type=jnp.float32).astype(jnp.bfloat16)
        adapter_piece = jnp.dot(tok_piece, down_piece, preferred_element_type=jnp.float32).astype(jnp.bfloat16)
        return (carry[0] + gate_piece.astype(jnp.float32), carry[1] + adapter_piece.astype(jnp.float32)), None

    start = (jnp.zeros((count, width), jnp.float32), jnp.zeros((count, rank), jnp.float32))
    (gate_sum, adapter_sum), _ = lax.scan(row_step, start, (tok_blocks, weight_blocks, down_blocks))
    adapter_in = adapter_sum.astype(jnp.bfloat16)
    gate = gate_sum + adapter_scale * jnp.dot(adapter_in, adapter_up, preferred_element_type=jnp.float32)
    grad_gate = gate_gradient(gate, hidden_grad, up_branch)

    col_block = width // N_COL
    grad_blocks = grad_gate.reshape(count, N_COL, col_block).transpose(1, 0, 2)
    weight_cols = weight.reshape(depth, N_COL, col_block).transpose(1, 0, 2)
    up_cols = adapter_up.reshape(rank, N_COL, col_block).transpose(1, 0, 2)
    down_float = adapter_down.astype(jnp.float32)

    def col_step(carry, pieces):
        grad_piece, weight_piece, up_piece = pieces
        back = adapter_scale * lax.dot_general(grad_piece, up_piece, (((1,), (1,)), ((), ())), preferred_element_type=jnp.float32)
        base = lax.dot_general(grad_piece, weight_piece, (((1,), (1,)), ((), ())), preferred_element_type=jnp.float32)
        low = jnp.dot(back, down_float.T, precision=lax.Precision.HIGHEST)
        input_piece = (base + low).astype(jnp.bfloat16)
        back_piece = back.astype(jnp.bfloat16)
        return (carry[0] + input_piece.astype(jnp.float32), carry[1] + back_piece.astype(jnp.float32)), None

    start_cols = (jnp.zeros((count, depth), jnp.float32), jnp.zeros((count, rank), jnp.float32))
    (input_sum, back_sum), _ = lax.scan(col_step, start_cols, (grad_blocks, weight_cols, up_cols))
    grad_tokens = input_sum.astype(jnp.bfloat16)
    back_half = back_sum.astype(jnp.bfloat16)
    token_count = jnp.float32(count)
    grad_down = lax.dot_general(tokens, back_half, (((0,), (0,)), ((), ())), preferred_element_type=jnp.float32) / token_count
    grad_up = adapter_scale * lax.dot_general(adapter_in, grad_gate, (((0,), (0,)), ((), ())), preferred_element_type=jnp.float32) / token_count
    return grad_tokens, grad_down, grad_up
```

```python
import jax
import jax.numpy as jnp
from jax import lax
from jax.experimental import pallas as pl
from jax.experimental.pallas import tpu as pltpu
from jax.sharding import PartitionSpec as P

MESH = pl.DeviceIdType.MESH
NX, NY, NZ = 4, 8, 8
OWN = 64
PD = 64
D = NZ * 2 * PD
F = 1664
E = F + 128
R = 64
CHUNKS = ((0, 512), (512, 1024), (1024, 1408), (1408, 1792))
GROUPS = ((0, 1, 7), (2, 6), (3, 5), (4,))
BLOCK_ORDER = (0, 1, 3, 2)
PEERS = (4, 3, 5, 2, 6, 1, 7)
f32 = jnp.float32
bf16 = jnp.bfloat16
NT = (((1,), (1,)), ((), ()))


def block_of(rel):
    return ((rel - 3) % 8) // 2, ((rel - 3) % 8) % 2


def kernel(
    tok_ref, codes_hbm, scale_ref, down_ref, up_ref, ub_hbm, hg_hbm,
    out_ref, gd_ref, gu_ref,
    codes, ub, hg, scale, W, G, xt, part,
    rs_snd, rs_rcv, GR, back, zfin,
    up_acc, xs_snd, xs_rcv, xg_snd, xg_rcv, gd_all,
    *rest,
):
    group_bufs, sems = rest[: 4 * 8], rest[4 * 8 :]
    (loc_sem, tok_s, tok_r, sib_s, sib_r, rs_s, rs_r, ag_s, ag_r,
     p_s, p_r, z_s, z_r, xs_s, xs_r, xg_s, xg_r, gd_s, gd_r) = sems
    x = lax.axis_index("dp")
    y = lax.axis_index("row")
    col = lax.axis_index("col")
    z = col // 2
    c = lax.rem(col, 2)
    sib = {"col": 2 * z + 1 - c}

    def yid(k):
        return {"row": lax.rem(y + k + NY, NY)}

    def zid(k):
        return {"col": 2 * lax.rem(z + k, NZ) + c}

    def xid(k):
        return {"dp": lax.rem(x + k, NX)}

    def owner(rel):
        return lax.rem(y + rel, NY)

    sent = []

    def send(src, dst, ss, rs, dev):
        cp = pltpu.make_async_remote_copy(
            src_ref=src, dst_ref=dst, send_sem=ss, recv_sem=rs, device_id=dev, device_id_type=MESH
        )
        cp.start()
        sent.append(cp)
        return cp

    loads = [
        pltpu.make_async_copy(codes_hbm, codes, loc_sem.at[0]),
        pltpu.make_async_copy(ub_hbm, ub, loc_sem.at[1]),
        pltpu.make_async_copy(hg_hbm, hg, loc_sem.at[2]),
    ]
    barrier = pltpu.get_barrier_semaphore()
    greet = [zid(k) for k in PEERS] + [yid(1), yid(-1)] + [xid(k) for k in (2, 1, 3)] + [sib]
    for dev in greet:
        pl.semaphore_signal(barrier, inc=1, device_id=dev, device_id_type=MESH)
    for ld in loads:
        ld.start()

    for b in range(4):
        o1 = lax.rem(y + 3 + 2 * b, NY)
        o2 = lax.rem(o1 + 1, NY)
        left = tok_ref[:, pl.ds(pl.multiple_of((o1 // 2) * 128, 128), 128)].astype(f32)
        right = tok_ref[:, pl.ds(pl.multiple_of((o2 // 2) * 128, 128), 128)].astype(f32)
        both = jnp.concatenate([left[:, 64:], right[:, :64]], axis=1)
        G[b, z, c] = jnp.where(lax.rem(o1, 2) == 1, both, left).astype(bf16)
    pl.semaphore_wait(barrier, len(greet))

    tok = {}
    for b in BLOCK_ORDER:
        for k in PEERS:
            tok[b, k] = send(G.at[b, z, c], G.at[b, z, c], tok_s.at[b, k - 1], tok_r.at[b, k - 1], zid(k))

    scale[...] = scale_ref[...].astype(f32)
    loads[0].wait()

    @pl.loop(0, NZ)
    def _(i):
        rows = pl.ds(pl.multiple_of(i * 128, 128), 128)
        dn = down_ref[:, rows].astype(f32).T
        dn2 = (2.0 * dn).astype(bf16)
        for lo, hi in ((0, 512), (512, 1024), (1024, 1664)):
            low = jnp.dot(dn2, up_ref[:, lo:hi], preferred_element_type=f32)
            w = codes[rows, lo:hi].astype(f32) * scale[pl.ds(i, 1), lo:hi] + low
            W[i, :, :, lo:hi] = w.astype(bf16).reshape(2, PD, hi - lo)
        W[i, :, :, F:E] = jnp.concatenate([dn, jnp.zeros_like(dn)], axis=1).astype(bf16).reshape(2, PD, 128)

    fwd = {}

    def forward(b):
        for k in PEERS:
            tok[b, k].wait_recv()
        fwd[b] = send(G.at[b, :, c], G.at[b, :, c], sib_s.at[b], sib_r.at[b], sib)

    def gemm1(b):
        fwd[b].wait_recv()
        xt[...] = G[b].reshape(D, 128).T

        @pl.loop(0, E // 256)
        def _(n):
            cols = pl.ds(pl.multiple_of(n * 256, 256), 256)
            p = jnp.dot(xt[...], W[:, :, :, cols].reshape(D, 256), preferred_element_type=f32)
            part[(3 + 2 * b) % 8, :, cols] = p[:64]
            part[(4 + 2 * b) % 8, :, cols] = p[64:]

    rs = {}

    def rs_step(step, q):
        lo, hi = CHUNKS[q]
        for d, sign in ((0, 1), (1, -1)):
            rel = (sign * (5 - step)) % 8
            half = slice(0, 32) if d == 0 else slice(32, 64)
            other = slice(32, 64) if d == 0 else slice(0, 32)
            dst = rs_snd.at[d, step - 1]
            if step == 1:
                rs_snd[d, 0, half, lo:hi] = part[rel, half, lo:hi].astype(bf16)
                src, tgt = dst.at[half, lo:hi], rs_rcv.at[d, 0, half, lo:hi]
            else:
                rs[d, step - 1, q].wait_recv()
                if step == 2:
                    rs_snd[d, 1, half, lo:hi] = (
                        part[rel, half, lo:hi] + rs_rcv[d, 0, half, lo:hi].astype(f32)
                    ).astype(bf16)
                    rs_snd[d, 1, other, lo:hi] = part[rel, other, lo:hi].astype(bf16)
                else:
                    rs_snd[d, step - 1, :, lo:hi] = (
                        part[rel, :, lo:hi] + rs_rcv[d, step - 2, :, lo:hi].astype(f32)
                    ).astype(bf16)
                src, tgt = dst.at[:, lo:hi], rs_rcv.at[d, step - 1, :, lo:hi]
            rs[d, step, q] = send(
                src, tgt, rs_s.at[d, step - 1, q], rs_r.at[d, step - 1, q], yid(sign)
            )

    def gating(q):
        lo, hi = CHUNKS[q]
        rs[0, 4, q].wait_recv()
        rs[1, 4, q].wait_recv()
        total = part[0, :, lo:hi] + rs_rcv[0, 3, :, lo:hi].astype(f32) + rs_rcv[1, 3, :, lo:hi].astype(f32)
        end = min(hi, F)
        gate = total[:, : end - lo]
        s = jax.nn.sigmoid(gate)
        product = hg[:, lo:end].astype(f32) * ub[:, lo:end].astype(f32)
        GR[y, :, lo:end] = (product * s * (1.0 + gate * (1.0 - s))).astype(bf16)
        if hi > F:
            GR[y, :, F:hi] = total[:, F - lo :].astype(bf16)

    ag = {}

    def ag_hop(hop, q):
        lo, hi = CHUNKS[q]
        for d, sign in ((0, 1), (1, -1)):
            if hop > 1:
                ag[d, hop - 1, q].wait_recv()
            o = owner((-sign * (hop - 1)) % 8)
            rows = slice(0, 64)
            if hop == 4:
                rows = slice(0, 32) if d == 0 else slice(32, 64)
            ref = GR.at[o, rows, lo:hi]
            ag[d, hop, q] = send(ref, ref, ag_s.at[d, hop - 1, q], ag_r.at[d, hop - 1, q], yid(sign))

    pair, zs, zb = {}, {}, {}

    def bufs(g):
        return group_bufs[8 * g : 8 * g + 8]

    def grads(g):
        return jnp.concatenate([GR[owner(rel), :, :F] for rel in GROUPS[g]], axis=0)

    def group_back(g):
        bsnd, brcv, bz, bzr = bufs(g)[4:]
        bk = lax.dot_general(up_ref[...], grads(g), NT, preferred_element_type=f32)
        bsnd[...] = 2.0 * bk
        pair[g, 0] = send(bsnd, brcv, p_s.at[g, 0], p_r.at[g, 0], sib)

    def group_other(g):
        psnd = bufs(g)[0]
        n = psnd.shape[-1]
        p = lax.dot_general(W[:, 1 - c, :, :F].reshape(512, F), grads(g), NT, preferred_element_type=f32)
        psnd[...] = p.astype(bf16).reshape(NZ, PD, n)
        pair[g, 1] = send(psnd, bufs(g)[1], p_s.at[g, 1], p_r.at[g, 1], sib)

    def group_back_z(g):
        bsnd, brcv, bz, bzr = bufs(g)[4:]
        pair[g, 0].wait_recv()
        n = bsnd.shape[-1]
        bz[...] = (bsnd[...] + brcv[...]).reshape(NZ, 8, n)
        for k in PEERS:
            zb[g, k] = send(
                bz.at[lax.rem(z + k, NZ)], bzr.at[k - 1], z_s.at[g, 0, k - 1], z_r.at[g, 0, k - 1], zid(k)
            )

    def group_own(g):
        psnd, prcv, zsnd, zrcv = bufs(g)[:4]
        n = psnd.shape[-1]
        p = lax.dot_general(W[:, c, :, :F].reshape(512, F), grads(g), NT, preferred_element_type=f32)
        pair[g, 1].wait_recv()
        zsnd[...] = (p.reshape(NZ, PD, n) + prcv[...].astype(f32)).astype(bf16)
        for k in PEERS:
            zs[g, k] = send(
                zsnd.at[lax.rem(z + k, NZ)], zrcv.at[k - 1], z_s.at[g, 1, k - 1], z_r.at[g, 1, k - 1], zid(k)
            )

    def group_back_end(g):
        bz, bzr = bufs(g)[6:]
        total = bz[z]
        for k in PEERS:
            zb[g, k].wait_recv()
            total = total + bzr[k - 1]
        for i, rel in enumerate(GROUPS[g]):
            b, h = block_of(rel)
            back[b, :, h * 64 : h * 64 + 64] = total[:, i * 64 : i * 64 + 64]

    def group_end(g):
        zsnd, zrcv = bufs(g)[2:4]
        total = zsnd[z].astype(f32)
        for k in PEERS:
            zs[g, k].wait_recv()
            total = total + zrcv[k - 1].astype(f32)
        for i, rel in enumerate(GROUPS[g]):
            zfin[rel] = total[:, i * 64 : i * 64 + 64]

    forward(0)
    gemm1(0)
    forward(1)
    for q in range(4):
        rs_step(1, q)
    gemm1(1)
    forward(3)
    for q in range(4):
        rs_step(2, q)
    gemm1(3)
    forward(2)
    for q in range(4):
        rs_step(3, q)
    gemm1(2)
    for q in range(4):
        rs_step(4, q)
    loads[1].wait()
    loads[2].wait()

    for q in range(4):
        gating(q)
        ag_hop(1, q)
    for q in range(4):
        ag_hop(2, q)
    work = [group_back, group_other, group_back_z, group_own]
    for q in range(4):
        ag_hop(3, q)
        work[q](0)
    for q in range(4):
        ag_hop(4, q)
        work[q](1)
    for q in range(4):
        work[q](2)
    group_back_end(0)
    group_end(0)

    xs, xg = {}, {}
    adapter = None
    for q in (3, 2, 1, 0):
        ag[0, 4, q].wait_recv()
        ag[1, 4, q].wait_recv()
    adapter = GR[:, :, F:E].reshape(512, 128).astype(f32).T[:R].astype(bf16)
    for q in range(4):
        lo, hi = CHUNKS[q][0], min(CHUNKS[q][1], F)
        u = jnp.dot(adapter, GR[:, :, lo:hi].reshape(512, hi - lo), preferred_element_type=f32)
        u = (u * (2.0 / 2048.0)).reshape(NX, 16, hi - lo)
        up_acc[:, :, lo:hi] = u
        xs_snd[:, :, lo:hi] = u.astype(bf16)
        for k in (2, 1, 3):
            xs[k, q] = send(
                xs_snd.at[lax.rem(x + k, NX), :, lo:hi], xs_rcv.at[k - 1, :, lo:hi],
                xs_s.at[k - 1, q], xs_r.at[k - 1, q], xid(k),
            )
    for q in range(4):
        work[q](3)
    for g in (1, 2):
        group_back_end(g)
        group_end(g)
    for q in range(4):
        lo, hi = CHUNKS[q][0], min(CHUNKS[q][1], F)
        total = up_acc[x, :, lo:hi]
        for k in (1, 2, 3):
            xs[k, q].wait_recv()
            total = total + xs_rcv[k - 1, :, lo:hi].astype(f32)
        xg_snd[:, lo:hi] = total.astype(bf16)
        for k in (2, 1, 3):
            xg[k, q] = send(
                xg_snd.at[:, lo:hi], xg_rcv.at[k - 1, :, lo:hi],
                xg_s.at[k - 1, q], xg_r.at[k - 1, q], xid(k),
            )

    group_back_end(3)
    gd = jnp.zeros((8, D), f32)
    for b in range(4):
        gd = gd + lax.dot_general(
            back[b].astype(bf16), G[b].reshape(D, 128), NT, preferred_element_type=f32
        )
    gd_all[x] = gd * (1.0 / 2048.0)
    gds = [
        send(gd_all.at[x], gd_all.at[x], gd_s.at[k - 1], gd_r.at[k - 1], xid(k)) for k in (2, 1, 3)
    ]

    group_end(3)
    for i in range(4):
        a = zfin[lax.rem(2 * i - y + NY, NY)]
        b = zfin[lax.rem(2 * i + 1 - y + NY, NY)]
        out_ref[:, i * 128 : i * 128 + 128] = jnp.concatenate([a, b], axis=1).astype(bf16)

    for q in range(4):
        for k in (1, 2, 3):
            xg[k, q].wait_recv()
    gu_ref[x] = xg_snd[...].astype(f32)
    for k in (1, 2, 3):
        gu_ref[lax.rem(x - k + NX, NX)] = xg_rcv[k - 1].astype(f32)
    for cp in gds:
        cp.wait_recv()
    gd = gd_all[0] + gd_all[1] + gd_all[2] + gd_all[3]
    gd_ref[...] = jnp.where(c == 0, gd[:4], gd[4:])
    for cp in sent:
        cp.wait_send()


def group_scratch(n):
    return [
        pltpu.VMEM((NZ, PD, n), bf16),
        pltpu.VMEM((NZ, PD, n), bf16),
        pltpu.VMEM((NZ, PD, n), bf16),
        pltpu.VMEM((NZ - 1, PD, n), bf16),
        pltpu.VMEM((R, n), f32),
        pltpu.VMEM((R, n), f32),
        pltpu.VMEM((NZ, 8, n), f32),
        pltpu.VMEM((NZ - 1, 8, n), f32),
    ]


def per_device(tokens, codes, scales, down, up, up_branch, hidden_grad):
    vmem = pl.BlockSpec(memory_space=pltpu.VMEM)
    hbm = pl.BlockSpec(memory_space=pl.ANY)
    dma = pltpu.SemaphoreType.DMA
    scratch = [
        pltpu.VMEM((D, F), bf16),
        pltpu.VMEM((OWN, F), bf16),
        pltpu.VMEM((OWN, F), bf16),
        pltpu.VMEM((8, F), f32),
        pltpu.VMEM((NZ, 2, PD, E), bf16),
        pltpu.VMEM((4, NZ, 2, PD, 128), bf16),
        pltpu.VMEM((128, D), bf16),
        pltpu.VMEM((NY, OWN, E), f32),
        pltpu.VMEM((2, 4, OWN, E), bf16),
        pltpu.VMEM((2, 4, OWN, E), bf16),
        pltpu.VMEM((NY, OWN, E), bf16),
        pltpu.VMEM((4, 8, 128), f32),
        pltpu.VMEM((NY, PD, OWN), f32),
        pltpu.VMEM((NX, 16, F), f32),
        pltpu.VMEM((NX, 16, F), bf16),
        pltpu.VMEM((NX - 1, 16, F), bf16),
        pltpu.VMEM((16, F), bf16),
        pltpu.VMEM((NX - 1, 16, F), bf16),
        pltpu.VMEM((NX, 8, D), f32),
    ]
    for g in GROUPS:
        scratch += group_scratch(64 * len(g))
    scratch += [
        dma((3,)),
        dma((4, 7)), dma((4, 7)),
        dma((4,)), dma((4,)),
        dma((2, 4, 4)), dma((2, 4, 4)),
        dma((2, 4, 4)), dma((2, 4, 4)),
        dma((4, 2)), dma((4, 2)),
        dma((4, 2, 7)), dma((4, 2, 7)),
        dma((3, 4)), dma((3, 4)),
        dma((3, 4)), dma((3, 4)),
        dma((3,)), dma((3,)),
    ]
    out_t, gd_t, gu = pl.pallas_call(
        kernel,
        out_shape=(
            jax.ShapeDtypeStruct((PD, 512), bf16),
            jax.ShapeDtypeStruct((4, D), f32),
            jax.ShapeDtypeStruct((NX, 16, F), f32),
        ),
        in_specs=[vmem, hbm, vmem, vmem, vmem, hbm, hbm],
        out_specs=(vmem, vmem, vmem),
        scratch_shapes=scratch,
        compiler_params=pltpu.CompilerParams(
            collective_id=0, has_side_effects=True, vmem_limit_bytes=56 << 20
        ),
    )(tokens.T, codes, scales, down.T, up, up_branch, hidden_grad)
    return out_t.T, gd_t.T, gu.reshape(R, F)


def solution(mesh):
    return jax.shard_map(
        per_device,
        mesh=mesh,
        in_specs=(
            P("dp", ("row", "col")),
            P("row", "col"),
            P("row", "col"),
            P("row", None),
            P(None, "col"),
            P(("dp", "row"), "col"),
            P(("dp", "row"), "col"),
        ),
        out_specs=(P("dp", ("row", "col")), P("row", "col"), P(None, "col")),
        check_vma=False,
    )
```

```python
import jax
import jax.numpy as jnp
from jax import lax
from jax.experimental import pallas as pl
from jax.experimental.pallas import tpu as pltpu
from jax.sharding import PartitionSpec as P

MESH = pl.DeviceIdType.MESH
NX, NY, NZ = 4, 8, 8
OWN = 64
PD = 64
D = NZ * 2 * PD
F = 1664
A = 128
E = A + F
R = 64
CHUNKS = ((0, 512), (512, 1024), (1024, 1408), (1408, 1792))
GROUPS = ((0, 1, 7), (2, 6), (3, 5), (4,))
BLOCK_ORDER = (0, 1, 3, 2)
PEERS = (4, 3, 5, 2, 6, 1, 7)
f32 = jnp.float32
bf16 = jnp.bfloat16
NT = (((1,), (1,)), ((), ()))


def block_of(rel):
    return ((rel - 3) % 8) // 2, ((rel - 3) % 8) % 2


def kernel(
    tok_hbm, codes_hbm, scale_hbm, down_hbm, up_hbm, ub_hbm, hg_hbm,
    out_ref, gd_ref, gu_ref,
    tok_ref, codes, scale_ref, down_ref, up_ref, ub, hg, scale, W, G, xt, part,
    rs_snd, rs_rcv, GR, back, zfin,
    at_ref, up_acc, xs_snd, xs_rcv, xg_snd, xg_rcv, gd_all,
    *rest,
):
    group_bufs, sems = rest[: 4 * 8], rest[4 * 8 :]
    (loc_sem, tok_s, tok_r, sib_s, sib_r, rs_s, rs_r, ag_s, ag_r,
     p_s, p_r, z_s, z_r, xs_s, xs_r, xg_s, xg_r, gd_s, gd_r) = sems
    x = lax.axis_index("dp")
    y = lax.axis_index("row")
    col = lax.axis_index("col")
    z = col // 2
    c = lax.rem(col, 2)
    sib = {"col": 2 * z + 1 - c}

    def yid(k):
        return {"row": lax.rem(y + k + NY, NY)}

    def zid(k):
        return {"col": 2 * lax.rem(z + k, NZ) + c}

    def xid(k):
        return {"dp": lax.rem(x + k, NX)}

    def owner(rel):
        return lax.rem(y + rel, NY)

    sent = []

    def drain(keep=0):
        done = sent[: len(sent) - keep]
        del sent[: len(done)]
        for cp in done:
            cp.wait_send()

    def send(src, dst, ss, rs, dev):
        cp = pltpu.make_async_remote_copy(
            src_ref=src, dst_ref=dst, send_sem=ss, recv_sem=rs, device_id=dev, device_id_type=MESH
        )
        cp.start()
        sent.append(cp)
        return cp

    loads = [
        pltpu.make_async_copy(src, dst, loc_sem.at[i])
        for i, (src, dst) in enumerate((
            (tok_hbm, tok_ref), (down_hbm, down_ref), (up_hbm, up_ref), (scale_hbm, scale_ref),
            (codes_hbm, codes), (ub_hbm, ub), (hg_hbm, hg),
        ))
    ]
    barrier = pltpu.get_barrier_semaphore()
    greet = [zid(k) for k in PEERS] + [yid(1), yid(-1)] + [xid(k) for k in (2, 1, 3)] + [sib]
    for dev in greet:
        pl.semaphore_signal(barrier, inc=1, device_id=dev, device_id_type=MESH)
    for ld in loads:
        ld.start()
    loads[0].wait()

    for b in range(4):
        o1 = lax.rem(y + 3 + 2 * b, NY)
        o2 = lax.rem(o1 + 1, NY)
        left = tok_ref[:, pl.ds(pl.multiple_of((o1 // 2) * 128, 128), 128)].astype(f32)
        right = tok_ref[:, pl.ds(pl.multiple_of((o2 // 2) * 128, 128), 128)].astype(f32)
        both = jnp.concatenate([left[:, 64:], right[:, :64]], axis=1)
        G[b, z, c] = jnp.where(lax.rem(o1, 2) == 1, both, left).astype(bf16)
    pl.semaphore_wait(barrier, len(greet))

    tok = {}

    def spread(b):
        for k in PEERS:
            tok[b, k] = send(G.at[b, z, c], G.at[b, z, c], tok_s.at[b, k - 1], tok_r.at[b, k - 1], zid(k))

    spread(0)
    spread(1)

    for ld in loads[1:5]:
        ld.wait()
    scale[...] = scale_ref[...].astype(f32)

    @pl.loop(0, NZ)
    def _(i):
        rows = pl.ds(pl.multiple_of(i * 128, 128), 128)
        dn = down_ref[:, rows].astype(f32).T
        dn2 = (2.0 * dn).astype(bf16)
        for lo, hi in ((0, 512), (512, 1024), (1024, 1664)):
            low = jnp.dot(dn2, up_ref[:, lo:hi], preferred_element_type=f32)
            w = codes[rows, lo:hi].astype(f32) * scale[pl.ds(i, 1), lo:hi] + low
            W[i, :, :, A + lo : A + hi] = w.astype(bf16).reshape(2, PD, hi - lo)
        W[i, :, :, :A] = jnp.concatenate([dn, jnp.zeros_like(dn)], axis=1).astype(bf16).reshape(2, PD, 128)

    spread(3)
    spread(2)

    fwd = {}

    def forward(b):
        for k in PEERS:
            tok[b, k].wait_recv()
        fwd[b] = send(G.at[b, :, c], G.at[b, :, c], sib_s.at[b], sib_r.at[b], sib)

    def landed(b):
        fwd[b].wait_recv()
        xt[...] = G[b].reshape(D, 128).T

    def gemm1(b, q):
        lo, hi = CHUNKS[q]
        p = jnp.dot(xt[...], W[:, :, :, lo:hi].reshape(D, hi - lo), preferred_element_type=f32)
        part[(3 + 2 * b) % 8, :, lo:hi] = p[:64]
        part[(4 + 2 * b) % 8, :, lo:hi] = p[64:]

    rs = {}

    def rs_step(step, q):
        lo, hi = CHUNKS[q]
        for d, sign in ((0, 1), (1, -1)):
            rel = (sign * (5 - step)) % 8
            half = slice(0, 32) if d == 0 else slice(32, 64)
            other = slice(32, 64) if d == 0 else slice(0, 32)
            dst = rs_snd.at[d, step - 1]
            if step == 1:
                rs_snd[d, 0, half, lo:hi] = part[rel, half, lo:hi].astype(bf16)
                src, tgt = dst.at[half, lo:hi], rs_rcv.at[d, 0, half, lo:hi]
            else:
                rs[d, step - 1, q].wait_recv()
                if step == 2:
                    rs_snd[d, 1, half, lo:hi] = (
                        part[rel, half, lo:hi] + rs_rcv[d, 0, half, lo:hi].astype(f32)
                    ).astype(bf16)
                    rs_snd[d, 1, other, lo:hi] = part[rel, other, lo:hi].astype(bf16)
                else:
                    rs_snd[d, step - 1, :, lo:hi] = (
                        part[rel, :, lo:hi] + rs_rcv[d, step - 2, :, lo:hi].astype(f32)
                    ).astype(bf16)
                src, tgt = dst.at[:, lo:hi], rs_rcv.at[d, step - 1, :, lo:hi]
            rs[d, step, q] = send(
                src, tgt, rs_s.at[d, step - 1, q], rs_r.at[d, step - 1, q], yid(sign)
            )

    def gating(q):
        lo, hi = CHUNKS[q]
        rs[0, 4, q].wait_recv()
        rs[1, 4, q].wait_recv()
        total = part[0, :, lo:hi] + rs_rcv[0, 3, :, lo:hi].astype(f32) + rs_rcv[1, 3, :, lo:hi].astype(f32)
        at = max(lo, A)
        gate = total[:, at - lo :]
        s = jax.nn.sigmoid(gate)
        product = hg[:, at - A : hi - A].astype(f32) * ub[:, at - A : hi - A].astype(f32)
        GR[y, :, at:hi] = (product * s * (1.0 + gate * (1.0 - s))).astype(bf16)
        if lo < A:
            GR[y, :, lo:A] = total[:, : A - lo].astype(bf16)

    ag = {}

    def ag_hop(hop, q):
        lo, hi = CHUNKS[q]
        for d, sign in ((0, 1), (1, -1)):
            if hop > 1:
                ag[d, hop - 1, q].wait_recv()
            o = owner((-sign * (hop - 1)) % 8)
            rows = slice(0, 64)
            if hop == 4:
                rows = slice(0, 32) if d == 0 else slice(32, 64)
            ref = GR.at[o, rows, lo:hi]
            ag[d, hop, q] = send(ref, ref, ag_s.at[d, hop - 1, q], ag_r.at[d, hop - 1, q], yid(sign))

    pair, zs, zb = {}, {}, {}

    def bufs(g):
        return group_bufs[8 * g : 8 * g + 8]

    def grads(g):
        return jnp.concatenate([GR[owner(rel), :, A:] for rel in GROUPS[g]], axis=0)

    def group_back(g):
        bsnd, brcv, bz, bzr = bufs(g)[4:]
        bk = lax.dot_general(up_ref[...], grads(g), NT, preferred_element_type=f32)
        bsnd[...] = 2.0 * bk
        pair[g, 0] = send(bsnd, brcv, p_s.at[g, 0], p_r.at[g, 0], sib)

    def group_other(g):
        psnd = bufs(g)[0]
        n = psnd.shape[-1]
        p = lax.dot_general(W[:, 1 - c, :, A:].reshape(512, F), grads(g), NT, preferred_element_type=f32)
        psnd[...] = p.astype(bf16).reshape(NZ, PD, n)
        pair[g, 1] = send(psnd, bufs(g)[1], p_s.at[g, 1], p_r.at[g, 1], sib)

    def group_back_z(g):
        bsnd, brcv, bz, bzr = bufs(g)[4:]
        pair[g, 0].wait_recv()
        n = bsnd.shape[-1]
        bz[...] = (bsnd[...] + brcv[...]).reshape(NZ, 8, n)
        for k in PEERS:
            zb[g, k] = send(
                bz.at[lax.rem(z + k, NZ)], bzr.at[k - 1], z_s.at[g, 0, k - 1], z_r.at[g, 0, k - 1], zid(k)
            )

    def group_own(g):
        psnd, prcv, zsnd, zrcv = bufs(g)[:4]
        n = psnd.shape[-1]
        p = lax.dot_general(W[:, c, :, A:].reshape(512, F), grads(g), NT, preferred_element_type=f32)
        pair[g, 1].wait_recv()
        zsnd[...] = (p.reshape(NZ, PD, n) + prcv[...].astype(f32)).astype(bf16)
        for k in PEERS:
            zs[g, k] = send(
                zsnd.at[lax.rem(z + k, NZ)], zrcv.at[k - 1], z_s.at[g, 1, k - 1], z_r.at[g, 1, k - 1], zid(k)
            )

    def group_back_end(g):
        bz, bzr = bufs(g)[6:]
        total = bz[z]
        for k in PEERS:
            zb[g, k].wait_recv()
            total = total + bzr[k - 1]
        for i, rel in enumerate(GROUPS[g]):
            b, h = block_of(rel)
            back[b, :, h * 64 : h * 64 + 64] = total[:, i * 64 : i * 64 + 64]

    def group_end(g):
        zsnd, zrcv = bufs(g)[2:4]
        total = zsnd[z].astype(f32)
        for k in PEERS:
            zs[g, k].wait_recv()
            total = total + zrcv[k - 1].astype(f32)
        for i, rel in enumerate(GROUPS[g]):
            zfin[rel] = total[:, i * 64 : i * 64 + 64]

    forward(0)
    landed(0)
    for q in range(4):
        gemm1(0, q)
        rs_step(1, q)
    forward(1)
    landed(1)
    for q in range(4):
        gemm1(1, q)
    forward(3)
    for q in range(4):
        rs_step(2, q)
    landed(3)
    for q in range(4):
        gemm1(3, q)
    forward(2)
    for q in range(4):
        rs_step(3, q)
    landed(2)
    for q in range(4):
        gemm1(2, q)
    for q in range(4):
        rs_step(4, q)
    loads[5].wait()
    loads[6].wait()

    for q in range(4):
        gating(q)
        ag_hop(1, q)
    drain(16)
    for q in range(4):
        ag_hop(2, q)
    work = [group_back, group_other, group_back_z, group_own]
    for q in range(4):
        ag_hop(3, q)
        work[q](0)
    for q in range(4):
        ag_hop(4, q)
        work[q](1)

    xs, xg = {}, {}

    def last(q):
        ag[0, 4, q].wait_recv()
        ag[1, 4, q].wait_recv()

    def up_part(q):
        lo, hi = max(CHUNKS[q][0], A), CHUNKS[q][1]
        adapter = at_ref[...]
        u = jnp.dot(adapter, GR[:, :, lo:hi].reshape(512, hi - lo), preferred_element_type=f32)
        u = (u * (2.0 / 2048.0)).reshape(NX, 16, hi - lo)
        lo, hi = lo - A, hi - A
        up_acc[:, :, lo:hi] = u
        xs_snd[:, :, lo:hi] = u.astype(bf16)
        for k in (2, 1, 3):
            xs[k, q] = send(
                xs_snd.at[lax.rem(x + k, NX), :, lo:hi], xs_rcv.at[k - 1, :, lo:hi],
                xs_s.at[k - 1, q], xs_r.at[k - 1, q], xid(k),
            )

    def up_sum(q):
        lo, hi = max(CHUNKS[q][0], A) - A, CHUNKS[q][1] - A
        total = up_acc[x, :, lo:hi]
        for k in (1, 2, 3):
            xs[k, q].wait_recv()
            total = total + xs_rcv[k - 1, :, lo:hi].astype(f32)
        xg_snd[:, lo:hi] = total.astype(bf16)
        for k in (2, 1, 3):
            xg[k, q] = send(
                xg_snd.at[:, lo:hi], xg_rcv.at[k - 1, :, lo:hi],
                xg_s.at[k - 1, q], xg_r.at[k - 1, q], xid(k),
            )

    def down_part(blocks):
        total = jnp.zeros((8, D), f32)
        for b in blocks:
            total = total + lax.dot_general(
                back[b].astype(bf16), G[b].reshape(D, 128), NT, preferred_element_type=f32
            )
        return jnp.where(c == 0, total[:4], total[4:]) * (1.0 / 2048.0)

    group_back(2)
    last(0)
    at_ref[...] = GR[:, :, :A].reshape(512, A).astype(f32).T[:R].astype(bf16)
    up_part(0)
    group_other(2)
    last(1)
    up_part(1)
    group_back_z(2)
    group_own(2)
    last(2)
    up_part(2)
    last(3)
    group_back(3)
    up_part(3)
    group_other(3)
    group_back_z(3)
    group_own(3)
    for g in (0, 1):
        group_back_end(g)
        group_end(g)
    down_early = down_part((2, 3))
    group_back_end(2)
    for q in range(4):
        up_sum(q)

    group_back_end(3)
    gd_all[x] = down_early + down_part((0, 1))
    gds = [
        send(gd_all.at[x], gd_all.at[x], gd_s.at[k - 1], gd_r.at[k - 1], xid(k)) for k in (2, 1, 3)
    ]

    group_end(2)
    drain(24)
    group_end(3)
    for i in range(4):
        a = zfin[lax.rem(2 * i - y + NY, NY)]
        b = zfin[lax.rem(2 * i + 1 - y + NY, NY)]
        out_ref[:, i * 128 : i * 128 + 128] = jnp.concatenate([a, b], axis=1).astype(bf16)

    for q in range(4):
        for k in (1, 2, 3):
            xg[k, q].wait_recv()
    gu_ref[pl.ds(pl.multiple_of(x * 16, 16), 16), :] = xg_snd[...].astype(f32)
    for k in (1, 2, 3):
        at = pl.multiple_of(lax.rem(x - k + NX, NX) * 16, 16)
        gu_ref[pl.ds(at, 16), :] = xg_rcv[k - 1].astype(f32)
    for cp in gds:
        cp.wait_recv()
    gd_ref[...] = gd_all[0] + gd_all[1] + gd_all[2] + gd_all[3]
    drain()


def finish(out_ref, gd_ref, gu_ref, out_hbm, gd_hbm, gu_hbm, sem):
    copies = [
        pltpu.make_async_copy(src, dst, sem.at[i])
        for i, (src, dst) in enumerate(((gu_ref, gu_hbm), (out_ref, out_hbm), (gd_ref, gd_hbm)))
    ]
    for cp in copies:
        cp.start()
    for cp in copies:
        cp.wait()


def group_scratch(n):
    return [
        pltpu.VMEM((NZ, PD, n), bf16),
        pltpu.VMEM((NZ, PD, n), bf16),
        pltpu.VMEM((NZ, PD, n), bf16),
        pltpu.VMEM((NZ - 1, PD, n), bf16),
        pltpu.VMEM((R, n), f32),
        pltpu.VMEM((R, n), f32),
        pltpu.VMEM((NZ, 8, n), f32),
        pltpu.VMEM((NZ - 1, 8, n), f32),
    ]


def per_device(tokens, codes, scales, down, up, up_branch, hidden_grad):
    vmem = pl.BlockSpec(memory_space=pltpu.VMEM)
    hbm = pl.BlockSpec(memory_space=pl.ANY)
    dma = pltpu.SemaphoreType.DMA
    scratch = [
        pltpu.VMEM((PD, 512), bf16),
        pltpu.VMEM((D, F), bf16),
        pltpu.VMEM((8, F), bf16),
        pltpu.VMEM((R, D), bf16),
        pltpu.VMEM((R, F), bf16),
        pltpu.VMEM((OWN, F), bf16),
        pltpu.VMEM((OWN, F), bf16),
        pltpu.VMEM((8, F), f32),
        pltpu.VMEM((NZ, 2, PD, E), bf16),
        pltpu.VMEM((4, NZ, 2, PD, 128), bf16),
        pltpu.VMEM((128, D), bf16),
        pltpu.VMEM((NY, OWN, E), f32),
        pltpu.VMEM((2, 4, OWN, E), bf16),
        pltpu.VMEM((2, 4, OWN, E), bf16),
        pltpu.VMEM((NY, OWN, E), bf16),
        pltpu.VMEM((4, 8, 128), f32),
        pltpu.VMEM((NY, PD, OWN), f32),
        pltpu.VMEM((R, 512), bf16),
        pltpu.VMEM((NX, 16, F), f32),
        pltpu.VMEM((NX, 16, F), bf16),
        pltpu.VMEM((NX - 1, 16, F), bf16),
        pltpu.VMEM((16, F), bf16),
        pltpu.VMEM((NX - 1, 16, F), bf16),
        pltpu.VMEM((NX, 4, D), f32),
    ]
    for g in GROUPS:
        scratch += group_scratch(64 * len(g))
    scratch += [
        dma((7,)),
        dma((4, 7)), dma((4, 7)),
        dma((4,)), dma((4,)),
        dma((2, 4, 4)), dma((2, 4, 4)),
        dma((2, 4, 4)), dma((2, 4, 4)),
        dma((4, 2)), dma((4, 2)),
        dma((4, 2, 7)), dma((4, 2, 7)),
        dma((3, 4)), dma((3, 4)),
        dma((3, 4)), dma((3, 4)),
        dma((3,)), dma((3,)),
    ]
    shapes = (((PD, 512), bf16), ((4, D), f32), ((R, F), f32))
    parts = pl.pallas_call(
        kernel,
        out_shape=tuple(pltpu.VMEM(*s) for s in shapes),
        in_specs=[hbm] * 7,
        out_specs=(vmem,) * 3,
        scratch_shapes=scratch,
        compiler_params=pltpu.CompilerParams(
            collective_id=0, has_side_effects=True, vmem_limit_bytes=56 << 20
        ),
    )(tokens.T, codes, scales, down.T, up, up_branch, hidden_grad)
    out_t, gd_t, gu = pl.pallas_call(
        finish,
        out_shape=tuple(jax.ShapeDtypeStruct(*s) for s in shapes),
        in_specs=[hbm] * 3,
        out_specs=(hbm,) * 3,
        scratch_shapes=[dma((3,))],
    )(*(pltpu.with_memory_space_constraint(a, pltpu.VMEM) for a in parts))
    return out_t.T, gd_t.T, gu


def solution(mesh):
    return jax.shard_map(
        per_device,
        mesh=mesh,
        in_specs=(
            P("dp", ("row", "col")),
            P("row", "col"),
            P("row", "col"),
            P("row", None),
            P(None, "col"),
            P(("dp", "row"), "col"),
            P(("dp", "row"), "col"),
        ),
        out_specs=(P("dp", ("row", "col")), P("row", "col"), P(None, "col")),
        check_vma=False,
    )
```

```python
import jax
import jax.numpy as jnp
from jax import lax
from jax.experimental import pallas as pl
from jax.experimental.pallas import tpu as pltpu
from jax.sharding import PartitionSpec as P

MESH = pl.DeviceIdType.MESH
NX, NY, NZ = 4, 8, 8
OWN = 64
PD = 64
D = NZ * 2 * PD
F = 1664
R = 64
CHUNKS = ((0, 384), (384, 896), (896, 1280), (1280, 1664))
GROUPS = ((0, 1, 7), (2, 6), (3, 5), (4,))
PEERS = (4, 3, 5, 2, 6, 1, 7)
f32 = jnp.float32
bf16 = jnp.bfloat16
NT = (((1,), (1,)), ((), ()))


def block_of(rel):
    if rel in (4, 0):
        return 0, 0 if rel == 4 else 1
    return (4 - rel, 0) if rel < 4 else (rel - 4, 1)


def kernel(
    tok_hbm, codes_hbm, scale_hbm, down_hbm, up_hbm, ub_hbm, hg_hbm,
    out_ref, gd_ref, gu_ref,
    tok_ref, codes, scale_ref, down_ref, up_ref, ub, hg, scale, W, WA, G, PK, xt, part, part_a,
    rs_snd, rs_rcv, a_snd, a_rcv, GR, GA, GB, a_all, back, zfin,
    at_ref, up_acc, xs_snd, xs_rcv, xg_snd, xg_rcv, gd_all,
    *rest,
):
    group_bufs, sems = rest[: 4 * 8], rest[4 * 8 :]
    (loc_sem, tok_s, tok_r, sib_s, sib_r, rs_s, rs_r, ag_s, ag_r,
     ra_s, ra_r, ga_s, ga_r, ab_s, ab_r,
     p_s, p_r, z_s, z_r, xs_s, xs_r, xg_s, xg_r, gd_s, gd_r) = sems
    x = lax.axis_index("dp")
    y = lax.axis_index("row")
    col = lax.axis_index("col")
    z = col // 2
    c = lax.rem(col, 2)
    sib = {"col": 2 * z + 1 - c}

    def yid(k):
        return {"row": lax.rem(y + k + NY, NY)}

    def zid(k):
        return {"col": 2 * lax.rem(z + k, NZ) + c}

    def xid(k):
        return {"dp": lax.rem(x + k, NX)}

    def owner(rel):
        return lax.rem(y + rel, NY)

    sent = []

    def drain(keep=0):
        done = sent[: len(sent) - keep]
        del sent[: len(done)]
        for cp in done:
            cp.wait_send()

    def send(src, dst, ss, rs, dev):
        cp = pltpu.make_async_remote_copy(
            src_ref=src, dst_ref=dst, send_sem=ss, recv_sem=rs, device_id=dev, device_id_type=MESH
        )
        cp.start()
        sent.append(cp)
        return cp

    loads = [
        pltpu.make_async_copy(src, dst, loc_sem.at[i])
        for i, (src, dst) in enumerate((
            (tok_hbm, tok_ref), (down_hbm, down_ref), (up_hbm, up_ref), (scale_hbm, scale_ref),
            (codes_hbm, codes), (ub_hbm, ub), (hg_hbm, hg),
        ))
    ]
    barrier = pltpu.get_barrier_semaphore()
    greet = [zid(k) for k in PEERS] + [yid(1), yid(-1)] + [xid(k) for k in (2, 1, 3)] + [sib]
    for dev in greet:
        pl.semaphore_signal(barrier, inc=1, device_id=dev, device_id_type=MESH)
    for ld in loads:
        ld.start()
    loads[0].wait()

    def piece(rel):
        o = owner(rel)
        two = tok_ref[:, pl.ds(pl.multiple_of((o // 2) * 128, 128), 128)].astype(f32)
        return jnp.where(lax.rem(o, 2) == 1, two[:, 64:], two[:, :64])

    for j, rel in ((0, 4), (1, 0)):
        p = piece(rel)
        PK[j, z, c] = jnp.concatenate([p[:32], p[32:]], axis=1).astype(bf16)
    for b in (1, 2, 3):
        G[b, z, c] = jnp.concatenate([piece(4 - b), piece(4 + b)], axis=1).astype(bf16)
    pl.semaphore_wait(barrier, len(greet))

    def tokens_of(item):
        return PK.at[item // 4] if item in (0, 4) else G.at[item]

    tok = {}

    def spread(item):
        ref = tokens_of(item).at[z, c]
        for k in PEERS:
            tok[item, k] = send(ref, ref, tok_s.at[item, k - 1], tok_r.at[item, k - 1], zid(k))

    spread(0)
    spread(1)

    for ld in loads[1:5]:
        ld.wait()
    scale[...] = scale_ref[...].astype(f32)

    @pl.loop(0, NZ)
    def _(i):
        rows = pl.ds(pl.multiple_of(i * 128, 128), 128)
        dn = down_ref[:, rows].astype(f32).T
        dn2 = (2.0 * dn).astype(bf16)
        for lo, hi in ((0, 512), (512, 1024), (1024, 1664)):
            low = jnp.dot(dn2, up_ref[:, lo:hi], preferred_element_type=f32)
            w = codes[rows, lo:hi].astype(f32) * scale[pl.ds(i, 1), lo:hi] + low
            W[i, :, :, lo:hi] = w.astype(bf16).reshape(2, PD, hi - lo)
        WA[i] = jnp.concatenate([dn, jnp.zeros_like(dn)], axis=1).astype(bf16).reshape(2, PD, 128)

    for item in (2, 3, 4):
        spread(item)

    fwd = {}

    def forward(item):
        for k in PEERS:
            tok[item, k].wait_recv()
        ref = tokens_of(item).at[:, c]
        fwd[item] = send(ref, ref, sib_s.at[item], sib_r.at[item], sib)

    def landed(item):
        fwd[item].wait_recv()
        if item in (0, 4):
            xt[:, :512] = PK[item // 4].reshape(512, 128).T
        else:
            xt[...] = G[item].reshape(D, 128).T

    def times(item, w, lo, hi):
        if item in (0, 4):
            return jnp.dot(
                xt[:64, :512], w[:, :, :32, lo:hi].reshape(512, hi - lo), preferred_element_type=f32
            ) + jnp.dot(
                xt[64:, :512], w[:, :, 32:, lo:hi].reshape(512, hi - lo), preferred_element_type=f32
            )
        return jnp.dot(xt[...], w[:, :, :, lo:hi].reshape(D, hi - lo), preferred_element_type=f32)

    def rels(item):
        return (4 - item,) if item in (0, 4) else (4 - item, 4 + item)

    def gemm1(item, q):
        lo, hi = CHUNKS[q]
        p = times(item, W, lo, hi)
        for i, rel in enumerate(rels(item)):
            part[rel, :, lo:hi] = p[64 * i : 64 * i + 64]

    def gemm_a(item):
        p = times(item, WA, 0, 128)
        for i, rel in enumerate(rels(item)):
            part_a[rel] = p[64 * i : 64 * i + 64]

    def packed(rel):
        v = part_a[rel, pl.ds(pl.multiple_of(c * 32, 32), 32), :]
        return v[:16] + jnp.concatenate([v[16:, 64:], v[16:, :64]], axis=1)

    rs = {}

    def rs_step(step, q):
        lo, hi = CHUNKS[q]
        for d, sign in ((0, 1), (1, -1)):
            rel = (sign * (5 - step)) % 8
            half = slice(0, 32) if d == 0 else slice(32, 64)
            other = slice(32, 64) if d == 0 else slice(0, 32)
            dst = rs_snd.at[d, step - 1]
            if step == 1:
                rs_snd[d, 0, half, lo:hi] = part[rel, half, lo:hi].astype(bf16)
                src, tgt = dst.at[half, lo:hi], rs_rcv.at[d, 0, half, lo:hi]
            else:
                rs[d, step - 1, q].wait_recv()
                if step == 2:
                    rs_snd[d, 1, half, lo:hi] = (
                        part[rel, half, lo:hi] + rs_rcv[d, 0, half, lo:hi].astype(f32)
                    ).astype(bf16)
                    rs_snd[d, 1, other, lo:hi] = part[rel, other, lo:hi].astype(bf16)
                else:
                    rs_snd[d, step - 1, :, lo:hi] = (
                        part[rel, :, lo:hi] + rs_rcv[d, step - 2, :, lo:hi].astype(f32)
                    ).astype(bf16)
                src, tgt = dst.at[:, lo:hi], rs_rcv.at[d, step - 1, :, lo:hi]
            rs[d, step, q] = send(
                src, tgt, rs_s.at[d, step - 1, q], rs_r.at[d, step - 1, q], yid(sign)
            )

    ra = {}

    def rs_a(step):
        for d, sign in ((0, 1), (1, -1)):
            if d == 1 and step == 1:
                continue
            v = packed((sign * (5 - step)) % 8)
            if step > 1 + d:
                ra[d, step - 1].wait_recv()
                v = v + a_rcv[d, step - 2].astype(f32)
            a_snd[d, step - 1] = v.astype(bf16)
            ra[d, step] = send(
                a_snd.at[d, step - 1], a_rcv.at[d, step - 1],
                ra_s.at[d, step - 1], ra_r.at[d, step - 1], yid(sign),
            )

    def sum_a():
        ra[0, 4].wait_recv()
        ra[1, 4].wait_recv()
        GA[y] = (packed(0) + a_rcv[0, 3].astype(f32) + a_rcv[1, 3].astype(f32)).astype(bf16)

    ga = {}

    def ag_a(hop):
        for d, sign in ((0, 1), (1, -1)):
            if hop > 1:
                ga[d, hop - 1].wait_recv()
            if d == 1 and hop == 4:
                continue
            ref = GA.at[owner((-sign * (hop - 1)) % 8)]
            ga[d, hop] = send(ref, ref, ga_s.at[d, hop - 1], ga_r.at[d, hop - 1], yid(sign))

    def gating(q):
        lo, hi = CHUNKS[q]
        rs[0, 4, q].wait_recv()
        rs[1, 4, q].wait_recv()
        total = part[0, :, lo:hi] + rs_rcv[0, 3, :, lo:hi].astype(f32) + rs_rcv[1, 3, :, lo:hi].astype(f32)
        s = jax.nn.sigmoid(total)
        product = hg[:, lo:hi].astype(f32) * ub[:, lo:hi].astype(f32)
        GR[y, :, lo:hi] = (product * s * (1.0 + total * (1.0 - s))).astype(bf16)

    ag = {}

    def ag_hop(hop, q):
        lo, hi = CHUNKS[q]
        for d, sign in ((0, 1), (1, -1)):
            if hop > 1:
                ag[d, hop - 1, q].wait_recv()
            o = owner((-sign * (hop - 1)) % 8)
            rows = slice(0, 64)
            if hop == 4:
                rows = slice(0, 32) if d == 0 else slice(32, 64)
            ref = GR.at[o, rows, lo:hi]
            ag[d, hop, q] = send(ref, ref, ag_s.at[d, hop - 1, q], ag_r.at[d, hop - 1, q], yid(sign))

    pair, zs, zb = {}, {}, {}

    def bufs(g):
        return group_bufs[8 * g : 8 * g + 8]

    def grads(g):
        return jnp.concatenate([GR[owner(rel)] for rel in GROUPS[g]], axis=0)

    def group_back(g):
        bsnd, brcv, bz, bzr = bufs(g)[4:]
        bk = lax.dot_general(up_ref[...], grads(g), NT, preferred_element_type=f32)
        bsnd[...] = 2.0 * bk
        pair[g, 0] = send(bsnd, brcv, p_s.at[g, 0], p_r.at[g, 0], sib)

    def group_other(g):
        psnd = bufs(g)[0]
        n = psnd.shape[-1]
        p = lax.dot_general(W[:, 1 - c].reshape(512, F), grads(g), NT, preferred_element_type=f32)
        psnd[...] = p.astype(bf16).reshape(NZ, PD, n)
        pair[g, 1] = send(psnd, bufs(g)[1], p_s.at[g, 1], p_r.at[g, 1], sib)

    def group_back_z(g):
        bsnd, brcv, bz, bzr = bufs(g)[4:]
        pair[g, 0].wait_recv()
        n = bsnd.shape[-1]
        bz[...] = (bsnd[...] + brcv[...]).reshape(NZ, 8, n)
        for k in PEERS:
            zb[g, k] = send(
                bz.at[lax.rem(z + k, NZ)], bzr.at[k - 1], z_s.at[g, 0, k - 1], z_r.at[g, 0, k - 1], zid(k)
            )

    def group_own(g):
        psnd, prcv, zsnd, zrcv = bufs(g)[:4]
        n = psnd.shape[-1]
        p = lax.dot_general(W[:, c].reshape(512, F), grads(g), NT, preferred_element_type=f32)
        pair[g, 1].wait_recv()
        zsnd[...] = (p.reshape(NZ, PD, n) + prcv[...].astype(f32)).astype(bf16)
        for k in PEERS:
            zs[g, k] = send(
                zsnd.at[lax.rem(z + k, NZ)], zrcv.at[k - 1], z_s.at[g, 1, k - 1], z_r.at[g, 1, k - 1], zid(k)
            )

    def group_back_end(g):
        bz, bzr = bufs(g)[6:]
        total = bz[z]
        for k in PEERS:
            zb[g, k].wait_recv()
            total = total + bzr[k - 1]
        for i, rel in enumerate(GROUPS[g]):
            b, h = block_of(rel)
            back[b, :, h * 64 : h * 64 + 64] = total[:, i * 64 : i * 64 + 64]

    def group_end(g):
        zsnd, zrcv = bufs(g)[2:4]
        total = zsnd[z].astype(f32)
        for k in PEERS:
            zs[g, k].wait_recv()
            total = total + zrcv[k - 1].astype(f32)
        for i, rel in enumerate(GROUPS[g]):
            zfin[rel] = total[:, i * 64 : i * 64 + 64]

    forward(0)
    landed(0)
    for q in range(4):
        gemm1(0, q)
        rs_step(1, q)
        if q == 0:
            gemm_a(0)
            rs_a(1)
    for step in (2, 3, 4):
        if step == 2:
            forward(1)
        landed(step - 1)
        for q in range(4):
            gemm1(step - 1, q)
        gemm_a(step - 1)
        forward(step)
        for q in range(4):
            rs_step(step, q)
            if q == 0:
                rs_a(step)
    landed(4)
    for q in range(4):
        gemm1(4, q)
    gemm_a(4)
    loads[5].wait()
    loads[6].wait()

    for q in range(4):
        gating(q)
        ag_hop(1, q)
        if q == 0:
            sum_a()
            ag_a(1)
    drain(17)
    for q in range(4):
        ag_hop(2, q)
        if q == 0:
            ag_a(2)
    low, high = [
        jnp.concatenate([PK[0, :, :, :, h].astype(f32), PK[1, :, :, :, h].astype(f32)], axis=3).astype(bf16)
        for h in (slice(0, 64), slice(64, 128))
    ]
    G[0, :, :, :32, :] = low
    G[0, :, :, 32:, :] = high
    for hop, g in ((3, 0), (4, 1)):
        group_back(g)
        group_other(g)
        ag_hop(hop, 0)
        ag_a(hop)
        group_back_z(g)
        ag_hop(hop, 1)
        group_own(g)
        ag_hop(hop, 2)
        ag_hop(hop, 3)

    xs, xg = {}, {}

    def last(q):
        ag[0, 4, q].wait_recv()
        ag[1, 4, q].wait_recv()

    def up_part(q):
        lo, hi = CHUNKS[q]
        u = jnp.dot(at_ref[...], GR[:, :, lo:hi].reshape(512, hi - lo), preferred_element_type=f32)
        u = (u * (2.0 / 2048.0)).reshape(NX, 16, hi - lo)
        up_acc[:, :, lo:hi] = u
        xs_snd[:, :, lo:hi] = u.astype(bf16)
        for k in (2, 1, 3):
            xs[k, q] = send(
                xs_snd.at[lax.rem(x + k, NX), :, lo:hi], xs_rcv.at[k - 1, :, lo:hi],
                xs_s.at[k - 1, q], xs_r.at[k - 1, q], xid(k),
            )

    def up_sum(q):
        lo, hi = CHUNKS[q]
        total = up_acc[x, :, lo:hi]
        for k in (1, 2, 3):
            xs[k, q].wait_recv()
            total = total + xs_rcv[k - 1, :, lo:hi].astype(f32)
        xg_snd[:, lo:hi] = total.astype(bf16)
        for k in (2, 1, 3):
            xg[k, q] = send(
                xg_snd.at[:, lo:hi], xg_rcv.at[k - 1, :, lo:hi],
                xg_s.at[k - 1, q], xg_r.at[k - 1, q], xid(k),
            )

    def down_part(blocks):
        total = jnp.zeros((8, D), f32)
        for b in blocks:
            total = total + lax.dot_general(
                back[b].astype(bf16), G[b].reshape(D, 128), NT, preferred_element_type=f32
            )
        return jnp.where(c == 0, total[:4], total[4:]) * (1.0 / 2048.0)

    group_back(2)
    group_other(2)
    ga[0, 4].wait_recv()
    swap = send(GA, GB, ab_s, ab_r, sib)
    last(0)
    group_back_z(2)
    group_own(2)
    swap.wait_recv()
    for half, src in ((c, GA), (1 - c, GB)):
        v = src[...].astype(f32)
        a_all[:, 2 * half] = v[:, :, :64]
        a_all[:, 2 * half + 1] = v[:, :, 64:]
    at_ref[...] = a_all[...].reshape(512, R).T.astype(bf16)
    up_part(0)
    last(1)
    up_part(1)
    last(2)
    up_part(2)
    last(3)
    group_back(3)
    group_other(3)
    up_part(3)
    group_back_z(3)
    group_own(3)
    for g in (0, 1):
        group_back_end(g)
        group_end(g)
    group_back_end(2)
    down_early = down_part((1, 2, 3))
    for q in range(4):
        up_sum(q)

    group_back_end(3)
    gd_all[x] = down_early + down_part((0,))
    gds = [
        send(gd_all.at[x], gd_all.at[x], gd_s.at[k - 1], gd_r.at[k - 1], xid(k)) for k in (2, 1, 3)
    ]

    group_end(2)
    drain(24)
    group_end(3)
    for i in range(4):
        a = zfin[lax.rem(2 * i - y + NY, NY)]
        b = zfin[lax.rem(2 * i + 1 - y + NY, NY)]
        out_ref[:, i * 128 : i * 128 + 128] = jnp.concatenate([a, b], axis=1).astype(bf16)

    for q in range(4):
        for k in (1, 2, 3):
            xg[k, q].wait_recv()
    gu_ref[pl.ds(pl.multiple_of(x * 16, 16), 16), :] = xg_snd[...].astype(f32)
    for k in (1, 2, 3):
        at = pl.multiple_of(lax.rem(x - k + NX, NX) * 16, 16)
        gu_ref[pl.ds(at, 16), :] = xg_rcv[k - 1].astype(f32)
    for cp in gds:
        cp.wait_recv()
    gd_ref[...] = gd_all[0] + gd_all[1] + gd_all[2] + gd_all[3]
    drain()


def finish(out_ref, gd_ref, gu_ref, out_hbm, gd_hbm, gu_hbm, sem):
    copies = [
        pltpu.make_async_copy(src, dst, sem.at[i])
        for i, (src, dst) in enumerate(((gu_ref, gu_hbm), (out_ref, out_hbm), (gd_ref, gd_hbm)))
    ]
    for cp in copies:
        cp.start()
    for cp in copies:
        cp.wait()


def group_scratch(n):
    return [
        pltpu.VMEM((NZ, PD, n), bf16),
        pltpu.VMEM((NZ, PD, n), bf16),
        pltpu.VMEM((NZ, PD, n), bf16),
        pltpu.VMEM((NZ - 1, PD, n), bf16),
        pltpu.VMEM((R, n), f32),
        pltpu.VMEM((R, n), f32),
        pltpu.VMEM((NZ, 8, n), f32),
        pltpu.VMEM((NZ - 1, 8, n), f32),
    ]


def per_device(tokens, codes, scales, down, up, up_branch, hidden_grad):
    vmem = pl.BlockSpec(memory_space=pltpu.VMEM)
    hbm = pl.BlockSpec(memory_space=pl.ANY)
    dma = pltpu.SemaphoreType.DMA
    scratch = [
        pltpu.VMEM((PD, 512), bf16),
        pltpu.VMEM((D, F), bf16),
        pltpu.VMEM((8, F), bf16),
        pltpu.VMEM((R, D), bf16),
        pltpu.VMEM((R, F), bf16),
        pltpu.VMEM((OWN, F), bf16),
        pltpu.VMEM((OWN, F), bf16),
        pltpu.VMEM((8, F), f32),
        pltpu.VMEM((NZ, 2, PD, F), bf16),
        pltpu.VMEM((NZ, 2, PD, 128), bf16),
        pltpu.VMEM((4, NZ, 2, PD, 128), bf16),
        pltpu.VMEM((2, NZ, 2, PD // 2, 128), bf16),
        pltpu.VMEM((128, D), bf16),
        pltpu.VMEM((NY, OWN, F), f32),
        pltpu.VMEM((NY, OWN, 128), f32),
        pltpu.VMEM((2, 4, OWN, F), bf16),
        pltpu.VMEM((2, 4, OWN, F), bf16),
        pltpu.VMEM((2, 4, 16, 128), bf16),
        pltpu.VMEM((2, 4, 16, 128), bf16),
        pltpu.VMEM((NY, OWN, F), bf16),
        pltpu.VMEM((NY, 16, 128), bf16),
        pltpu.VMEM((NY, 16, 128), bf16),
        pltpu.VMEM((NY, 4, 16, R), f32),
        pltpu.VMEM((4, 8, 128), f32),
        pltpu.VMEM((NY, PD, OWN), f32),
        pltpu.VMEM((R, 512), bf16),
        pltpu.VMEM((NX, 16, F), f32),
        pltpu.VMEM((NX, 16, F), bf16),
        pltpu.VMEM((NX - 1, 16, F), bf16),
        pltpu.VMEM((16, F), bf16),
        pltpu.VMEM((NX - 1, 16, F), bf16),
        pltpu.VMEM((NX, 4, D), f32),
    ]
    for g in GROUPS:
        scratch += group_scratch(64 * len(g))
    scratch += [
        dma((7,)),
        dma((5, 7)), dma((5, 7)),
        dma((5,)), dma((5,)),
        dma((2, 4, 4)), dma((2, 4, 4)),
        dma((2, 4, 4)), dma((2, 4, 4)),
        dma((2, 4)), dma((2, 4)),
        dma((2, 4)), dma((2, 4)),
        dma, dma,
        dma((4, 2)), dma((4, 2)),
        dma((4, 2, 7)), dma((4, 2, 7)),
        dma((3, 4)), dma((3, 4)),
        dma((3, 4)), dma((3, 4)),
        dma((3,)), dma((3,)),
    ]
    shapes = (((PD, 512), bf16), ((4, D), f32), ((R, F), f32))
    parts = pl.pallas_call(
        kernel,
        out_shape=tuple(pltpu.VMEM(*s) for s in shapes),
        in_specs=[hbm] * 7,
        out_specs=(vmem,) * 3,
        scratch_shapes=scratch,
        compiler_params=pltpu.CompilerParams(
            collective_id=0, has_side_effects=True, vmem_limit_bytes=56 << 20
        ),
    )(tokens.T, codes, scales, down.T, up, up_branch, hidden_grad)
    out_t, gd_t, gu = pl.pallas_call(
        finish,
        out_shape=tuple(jax.ShapeDtypeStruct(*s) for s in shapes),
        in_specs=[hbm] * 3,
        out_specs=(hbm,) * 3,
        scratch_shapes=[dma((3,))],
    )(*(pltpu.with_memory_space_constraint(a, pltpu.VMEM) for a in parts))
    return out_t.T, gd_t.T, gu


def solution(mesh):
    return jax.shard_map(
        per_device,
        mesh=mesh,
        in_specs=(
            P("dp", ("row", "col")),
            P("row", "col"),
            P("row", "col"),
            P("row", None),
            P(None, "col"),
            P(("dp", "row"), "col"),
            P(("dp", "row"), "col"),
        ),
        out_specs=(P("dp", ("row", "col")), P("row", "col"), P(None, "col")),
        check_vma=False,
    )
```

```python
import jax
import jax.numpy as jnp
from jax import lax
from jax.experimental import pallas as pl
from jax.experimental.pallas import tpu as pltpu
from jax.sharding import PartitionSpec as P

MESH = pl.DeviceIdType.MESH
NX, NY, NZ = 4, 8, 8
OWN = 64
PD = 64
D = NZ * 2 * PD
F = 1664
R = 64
CHUNKS = ((0, 256), (256, 768), (768, 1280), (1280, 1536), (1536, 1664))
Q = len(CHUNKS)
RS_ORDER = (4, 0, 1, 2, 3)
GROUPS = ((0, 1, 7), (2, 6), (3, 5), (4,))
PEERS = (4, 3, 5, 2, 6, 1, 7)
f32 = jnp.float32
bf16 = jnp.bfloat16
NT = (((1,), (1,)), ((), ()))


def block_of(rel):
    if rel in (4, 0):
        return 0, 0 if rel == 4 else 1
    return (4 - rel, 0) if rel < 4 else (rel - 4, 1)


def kernel(
    tok_hbm, codes_hbm, scale_hbm, down_hbm, up_hbm, ub_hbm, hg_hbm,
    out_ref, gd_ref, gu_ref,
    tok_ref, codes, scale_ref, down_ref, up_ref, ub, hg, scale, W, WA, G, PK, xt, part, part_a,
    rs_snd, rs_rcv, a_snd, a_rcv, GR, GA, GB, a_all, back, bk_snd, bk_rcv, bz_snd, bz_rcv, by_snd, by_rcv, zfin,
    at_ref, up_acc, xs_snd, xs_rcv, xg_snd, xg_rcv, gd_all,
    *rest,
):
    group_bufs, sems = rest[: 4 * 6], rest[4 * 6 :]
    (loc_sem, tok_s, tok_r, sib_s, sib_r, rs_s, rs_r, ag_s, ag_r,
     ra_s, ra_r, ga_s, ga_r, ab_s, ab_r,
     p_s, p_r, z_s, z_r, bp_s, bp_r, bz_s, bz_r, by_s, by_r, xs_s, xs_r, xg_s, xg_r, gd_s, gd_r) = sems
    x = lax.axis_index("dp")
    y = lax.axis_index("row")
    col = lax.axis_index("col")
    z = col // 2
    c = lax.rem(col, 2)
    sib = {"col": 2 * z + 1 - c}

    def yid(k):
        return {"row": lax.rem(y + k + NY, NY)}

    def zid(k):
        return {"col": 2 * lax.rem(z + k, NZ) + c}

    def xid(k):
        return {"dp": lax.rem(x + k, NX)}

    def owner(rel):
        return lax.rem(y + rel, NY)

    sent = []

    def drain(keep=0):
        done = sent[: len(sent) - keep]
        del sent[: len(done)]
        for cp in done:
            cp.wait_send()

    def send(src, dst, ss, rs, dev):
        cp = pltpu.make_async_remote_copy(
            src_ref=src, dst_ref=dst, send_sem=ss, recv_sem=rs, device_id=dev, device_id_type=MESH
        )
        cp.start()
        sent.append(cp)
        return cp

    loads = [
        pltpu.make_async_copy(src, dst, loc_sem.at[i])
        for i, (src, dst) in enumerate((
            (tok_hbm, tok_ref), (down_hbm, down_ref), (up_hbm, up_ref), (scale_hbm, scale_ref),
            (codes_hbm, codes), (ub_hbm, ub), (hg_hbm, hg),
        ))
    ]
    barrier = pltpu.get_barrier_semaphore()
    greet = [zid(k) for k in PEERS] + [yid(k) for k in PEERS] + [xid(k) for k in (2, 1, 3)] + [sib]
    for dev in greet:
        pl.semaphore_signal(barrier, inc=1, device_id=dev, device_id_type=MESH)
    for ld in loads:
        ld.start()
    loads[0].wait()

    def piece(rel):
        o = owner(rel)
        two = tok_ref[:, pl.ds(pl.multiple_of((o // 2) * 128, 128), 128)].astype(f32)
        return jnp.where(lax.rem(o, 2) == 1, two[:, 64:], two[:, :64])

    for j, rel in ((0, 4), (1, 0)):
        p = piece(rel)
        PK[j, z, c] = jnp.concatenate([p[:32], p[32:]], axis=1).astype(bf16)
    for b in (1, 2, 3):
        G[b, z, c] = jnp.concatenate([piece(4 - b), piece(4 + b)], axis=1).astype(bf16)
    pl.semaphore_wait(barrier, len(greet))

    def tokens_of(item):
        return PK.at[item // 4] if item in (0, 4) else G.at[item]

    tok = {}

    def spread(item):
        ref = tokens_of(item).at[z, c]
        for k in PEERS:
            tok[item, k] = send(ref, ref, tok_s.at[item, k - 1], tok_r.at[item, k - 1], zid(k))

    spread(0)
    spread(1)

    for ld in loads[1:5]:
        ld.wait()
    scale[...] = scale_ref[...].astype(f32)

    @pl.loop(0, NZ)
    def _(i):
        rows = pl.ds(pl.multiple_of(i * 128, 128), 128)
        dn = down_ref[:, rows].astype(f32).T
        dn2 = (2.0 * dn).astype(bf16)
        for lo, hi in ((0, 512), (512, 1024), (1024, 1664)):
            low = jnp.dot(dn2, up_ref[:, lo:hi], preferred_element_type=f32)
            w = codes[rows, lo:hi].astype(f32) * scale[pl.ds(i, 1), lo:hi] + low
            W[i, :, :, lo:hi] = w.astype(bf16).reshape(2, PD, hi - lo)
        WA[i] = jnp.concatenate([dn, jnp.zeros_like(dn)], axis=1).astype(bf16).reshape(2, PD, 128)

    for item in (2, 3, 4):
        spread(item)

    fwd = {}

    def forward(item):
        for k in PEERS:
            tok[item, k].wait_recv()
        ref = tokens_of(item).at[:, c]
        fwd[item] = send(ref, ref, sib_s.at[item], sib_r.at[item], sib)

    def landed(item):
        fwd[item].wait_recv()
        if item in (0, 4):
            xt[:, :512] = PK[item // 4].reshape(512, 128).T
        else:
            xt[...] = G[item].reshape(D, 128).T

    def times(item, w, lo, hi):
        if item in (0, 4):
            return jnp.dot(
                xt[:64, :512], w[:, :, :32, lo:hi].reshape(512, hi - lo), preferred_element_type=f32
            ) + jnp.dot(
                xt[64:, :512], w[:, :, 32:, lo:hi].reshape(512, hi - lo), preferred_element_type=f32
            )
        return jnp.dot(xt[...], w[:, :, :, lo:hi].reshape(D, hi - lo), preferred_element_type=f32)

    def rels(item):
        return (4 - item,) if item in (0, 4) else (4 - item, 4 + item)

    def gemm1(item, q):
        lo, hi = CHUNKS[q]
        p = times(item, W, lo, hi)
        for i, rel in enumerate(rels(item)):
            part[rel, :, lo:hi] = p[64 * i : 64 * i + 64]

    def gemm_a(item):
        p = times(item, WA, 0, 128)
        for i, rel in enumerate(rels(item)):
            part_a[rel] = p[64 * i : 64 * i + 64]

    def packed(rel):
        v = part_a[rel, pl.ds(pl.multiple_of(c * 32, 32), 32), :]
        return v[:16] + jnp.concatenate([v[16:, 64:], v[16:, :64]], axis=1)

    rs = {}

    def rs_step(step, q):
        lo, hi = CHUNKS[q]
        for d, sign in ((0, 1), (1, -1)):
            rel = (sign * (5 - step)) % 8
            half = slice(0, 32) if d == 0 else slice(32, 64)
            other = slice(32, 64) if d == 0 else slice(0, 32)
            dst = rs_snd.at[d, step - 1]
            if step == 1:
                rs_snd[d, 0, half, lo:hi] = part[rel, half, lo:hi].astype(bf16)
                src, tgt = dst.at[half, lo:hi], rs_rcv.at[d, 0, half, lo:hi]
            else:
                rs[d, step - 1, q].wait_recv()
                if step == 2:
                    rs_snd[d, 1, half, lo:hi] = (
                        part[rel, half, lo:hi] + rs_rcv[d, 0, half, lo:hi].astype(f32)
                    ).astype(bf16)
                    rs_snd[d, 1, other, lo:hi] = part[rel, other, lo:hi].astype(bf16)
                else:
                    rs_snd[d, step - 1, :, lo:hi] = (
                        part[rel, :, lo:hi] + rs_rcv[d, step - 2, :, lo:hi].astype(f32)
                    ).astype(bf16)
                src, tgt = dst.at[:, lo:hi], rs_rcv.at[d, step - 1, :, lo:hi]
            rs[d, step, q] = send(
                src, tgt, rs_s.at[d, step - 1, q], rs_r.at[d, step - 1, q], yid(sign)
            )

    ra = {}

    def rs_a(step):
        for d, sign in ((0, 1), (1, -1)):
            if d == 1 and step == 1:
                continue
            v = packed((sign * (5 - step)) % 8)
            if step > 1 + d:
                ra[d, step - 1].wait_recv()
                v = v + a_rcv[d, step - 2].astype(f32)
            a_snd[d, step - 1] = v.astype(bf16)
            ra[d, step] = send(
                a_snd.at[d, step - 1], a_rcv.at[d, step - 1],
                ra_s.at[d, step - 1], ra_r.at[d, step - 1], yid(sign),
            )

    def sum_a():
        ra[0, 4].wait_recv()
        ra[1, 4].wait_recv()
        GA[y] = (packed(0) + a_rcv[0, 3].astype(f32) + a_rcv[1, 3].astype(f32)).astype(bf16)

    ga = {}

    def ag_a(hop):
        for d, sign in ((0, 1), (1, -1)):
            if hop > 1:
                ga[d, hop - 1].wait_recv()
            if d == 1 and hop == 4:
                continue
            ref = GA.at[owner((-sign * (hop - 1)) % 8)]
            ga[d, hop] = send(ref, ref, ga_s.at[d, hop - 1], ga_r.at[d, hop - 1], yid(sign))

    def gating(q):
        lo, hi = CHUNKS[q]
        rs[0, 4, q].wait_recv()
        rs[1, 4, q].wait_recv()
        total = part[0, :, lo:hi] + rs_rcv[0, 3, :, lo:hi].astype(f32) + rs_rcv[1, 3, :, lo:hi].astype(f32)
        s = jax.nn.sigmoid(total)
        product = hg[:, lo:hi].astype(f32) * ub[:, lo:hi].astype(f32)
        GR[y, :, lo:hi] = (product * s * (1.0 + total * (1.0 - s))).astype(bf16)

    ag = {}

    def ag_hop(hop, q):
        lo, hi = CHUNKS[q]
        for d, sign in ((0, 1), (1, -1)):
            if hop > 1:
                ag[d, hop - 1, q].wait_recv()
            o = owner((-sign * (hop - 1)) % 8)
            rows = slice(0, 64)
            if hop == 4:
                rows = slice(0, 32) if d == 0 else slice(32, 64)
            ref = GR.at[o, rows, lo:hi]
            ag[d, hop, q] = send(ref, ref, ag_s.at[d, hop - 1, q], ag_r.at[d, hop - 1, q], yid(sign))

    bp, zb, yb = [], {}, {}

    def back_own():
        bk = lax.dot_general(up_ref[...], GR[y], NT, preferred_element_type=f32)
        bk_snd[...] = 2.0 * bk
        bp.append(send(bk_snd, bk_rcv, bp_s, bp_r, sib))

    def back_z():
        bp[0].wait_recv()
        bz_snd[...] = (bk_snd[...] + bk_rcv[...]).reshape(NZ, 8, OWN)
        for k in PEERS:
            zb[k] = send(
                bz_snd.at[lax.rem(z + k, NZ)], bz_rcv.at[k - 1], bz_s.at[k - 1], bz_r.at[k - 1], zid(k)
            )

    def back_y():
        total = bz_snd[z]
        for k in PEERS:
            zb[k].wait_recv()
            total = total + bz_rcv[k - 1]
        by_snd[...] = total
        for k in PEERS:
            yb[k] = send(by_snd, by_rcv.at[k - 1], by_s.at[k - 1], by_r.at[k - 1], yid(k))

    def back_end():
        for k in (0,) + PEERS:
            if k:
                yb[k].wait_recv()
            b, h = block_of((8 - k) % 8)
            back[b, :, h * 64 : h * 64 + 64] = by_rcv[k - 1] if k else by_snd[...]

    pair, zs = {}, {}

    def bufs(g):
        return group_bufs[6 * g : 6 * g + 6]

    def group_add(g, q):
        lo, hi = CHUNKS[q]
        n = 64 * len(GROUPS[g])
        gr = jnp.concatenate([GR[owner(rel), :, lo:hi] for rel in GROUPS[g]], axis=0)
        for ref, core in zip(bufs(g)[4:], (1 - c, c)):
            term = lax.dot_general(
                W[:, core, :, lo:hi].reshape(512, hi - lo), gr, NT, preferred_element_type=f32
            ).reshape(NZ, PD, n)
            ref[...] = term if q == 0 else ref[...] + term

    def group_pair(g):
        psnd, prcv = bufs(g)[:2]
        psnd[...] = bufs(g)[4][...].astype(bf16)
        pair[g] = send(psnd, prcv, p_s.at[g], p_r.at[g], sib)

    def group_own(g):
        _, prcv, zsnd, zrcv, _, own = bufs(g)
        pair[g].wait_recv()
        zsnd[...] = (own[...] + prcv[...].astype(f32)).astype(bf16)
        for k in PEERS:
            zs[g, k] = send(
                zsnd.at[lax.rem(z + k, NZ)], zrcv.at[k - 1], z_s.at[g, k - 1], z_r.at[g, k - 1], zid(k)
            )

    def group_end(g):
        zsnd, zrcv = bufs(g)[2:4]
        total = zsnd[z].astype(f32)
        for k in PEERS:
            zs[g, k].wait_recv()
            total = total + zrcv[k - 1].astype(f32)
        for i, rel in enumerate(GROUPS[g]):
            zfin[rel] = total[:, i * 64 : i * 64 + 64]

    forward(0)
    landed(0)
    for i, q in enumerate(RS_ORDER):
        gemm1(0, q)
        rs_step(1, q)
        if i == 1:
            gemm_a(0)
            rs_a(1)
    for step in (2, 3, 4):
        if step == 2:
            forward(1)
        landed(step - 1)
        for q in RS_ORDER:
            gemm1(step - 1, q)
        gemm_a(step - 1)
        forward(step)
        for i, q in enumerate(RS_ORDER):
            rs_step(step, q)
            if i == 1:
                rs_a(step)
    landed(4)
    for q in RS_ORDER:
        gemm1(4, q)
    gemm_a(4)
    loads[5].wait()
    loads[6].wait()

    gating(4)
    for q in range(Q):
        if q < 4:
            gating(q)
        ag_hop(1, q)
        if q == 0:
            sum_a()
            ag_a(1)
    back_own()
    drain(19)
    low, high = [
        jnp.concatenate([PK[0, :, :, :, h].astype(f32), PK[1, :, :, :, h].astype(f32)], axis=3).astype(bf16)
        for h in (slice(0, 64), slice(64, 128))
    ]
    G[0, :, :, :32, :] = low
    G[0, :, :, 32:, :] = high
    for hop, g in ((2, 0), (3, 1), (4, 2)):
        for q in range(Q):
            ag_hop(hop, q)
            if q == 0:
                ag_a(hop)
            group_add(g, q)
            if g > 0 and q == 0:
                group_own(g - 1)
            if g == 0 and q == 1:
                back_z()
            if g == 1 and q == 2:
                back_y()
        group_pair(g)

    xs, xg = {}, {}

    def last(q):
        ag[0, 4, q].wait_recv()
        ag[1, 4, q].wait_recv()

    def up_part(q):
        lo, hi = CHUNKS[q]
        u = jnp.dot(at_ref[...], GR[:, :, lo:hi].reshape(512, hi - lo), preferred_element_type=f32)
        u = (u * (2.0 / 2048.0)).reshape(NX, 16, hi - lo)
        up_acc[:, :, lo:hi] = u
        xs_snd[:, :, lo:hi] = u.astype(bf16)
        for k in (2, 1, 3):
            xs[k, q] = send(
                xs_snd.at[lax.rem(x + k, NX), :, lo:hi], xs_rcv.at[k - 1, :, lo:hi],
                xs_s.at[k - 1, q], xs_r.at[k - 1, q], xid(k),
            )

    def up_sum(q):
        lo, hi = CHUNKS[q]
        total = up_acc[x, :, lo:hi]
        for k in (1, 2, 3):
            xs[k, q].wait_recv()
            total = total + xs_rcv[k - 1, :, lo:hi].astype(f32)
        xg_snd[:, lo:hi] = total.astype(bf16)
        for k in (2, 1, 3):
            xg[k, q] = send(
                xg_snd.at[:, lo:hi], xg_rcv.at[k - 1, :, lo:hi],
                xg_s.at[k - 1, q], xg_r.at[k - 1, q], xid(k),
            )

    ga[0, 4].wait_recv()
    swap = send(GA, GB, ab_s, ab_r, sib)
    last(0)
    group_add(3, 0)
    group_own(2)
    swap.wait_recv()
    for half, src in ((c, GA), (1 - c, GB)):
        v = src[...].astype(f32)
        a_all[:, 2 * half] = v[:, :, :64]
        a_all[:, 2 * half + 1] = v[:, :, 64:]
    at_ref[...] = a_all[...].reshape(512, R).T.astype(bf16)
    up_part(0)
    for q in range(1, Q):
        last(q)
        group_add(3, q)
        if q < Q - 1:
            up_part(q)
    group_pair(3)
    up_part(Q - 1)
    group_own(3)

    back_end()
    gd = jnp.zeros((8, D), f32)
    for b in range(4):
        gd = gd + lax.dot_general(back[b].astype(bf16), G[b].reshape(D, 128), NT, preferred_element_type=f32)
    gd_all[x] = jnp.where(c == 0, gd[:4], gd[4:]) * (1.0 / 2048.0)
    gds = [
        send(gd_all.at[x], gd_all.at[x], gd_s.at[k - 1], gd_r.at[k - 1], xid(k)) for k in (2, 1, 3)
    ]
    group_end(0)
    group_end(1)
    for q in range(Q):
        up_sum(q)

    group_end(2)
    drain(24)
    group_end(3)
    for i in range(4):
        a = zfin[lax.rem(2 * i - y + NY, NY)]
        b = zfin[lax.rem(2 * i + 1 - y + NY, NY)]
        out_ref[:, i * 128 : i * 128 + 128] = jnp.concatenate([a, b], axis=1).astype(bf16)

    for q in range(Q):
        for k in (1, 2, 3):
            xg[k, q].wait_recv()
    gu_ref[pl.ds(pl.multiple_of(x * 16, 16), 16), :] = xg_snd[...].astype(f32)
    for k in (1, 2, 3):
        at = pl.multiple_of(lax.rem(x - k + NX, NX) * 16, 16)
        gu_ref[pl.ds(at, 16), :] = xg_rcv[k - 1].astype(f32)
    for cp in gds:
        cp.wait_recv()
    gd_ref[...] = gd_all[0] + gd_all[1] + gd_all[2] + gd_all[3]
    drain()


def finish(out_ref, gd_ref, gu_ref, out_hbm, gd_hbm, gu_hbm, sem):
    copies = [
        pltpu.make_async_copy(src, dst, sem.at[i])
        for i, (src, dst) in enumerate(((gu_ref, gu_hbm), (out_ref, out_hbm), (gd_ref, gd_hbm)))
    ]
    for cp in copies:
        cp.start()
    for cp in copies:
        cp.wait()


def group_scratch(n):
    return [
        pltpu.VMEM((NZ, PD, n), bf16),
        pltpu.VMEM((NZ, PD, n), bf16),
        pltpu.VMEM((NZ, PD, n), bf16),
        pltpu.VMEM((NZ - 1, PD, n), bf16),
        pltpu.VMEM((NZ, PD, n), f32),
        pltpu.VMEM((NZ, PD, n), f32),
    ]


def per_device(tokens, codes, scales, down, up, up_branch, hidden_grad):
    vmem = pl.BlockSpec(memory_space=pltpu.VMEM)
    hbm = pl.BlockSpec(memory_space=pl.ANY)
    dma = pltpu.SemaphoreType.DMA
    scratch = [
        pltpu.VMEM((PD, 512), bf16),
        pltpu.VMEM((D, F), bf16),
        pltpu.VMEM((8, F), bf16),
        pltpu.VMEM((R, D), bf16),
        pltpu.VMEM((R, F), bf16),
        pltpu.VMEM((OWN, F), bf16),
        pltpu.VMEM((OWN, F), bf16),
        pltpu.VMEM((8, F), f32),
        pltpu.VMEM((NZ, 2, PD, F), bf16),
        pltpu.VMEM((NZ, 2, PD, 128), bf16),
        pltpu.VMEM((4, NZ, 2, PD, 128), bf16),
        pltpu.VMEM((2, NZ, 2, PD // 2, 128), bf16),
        pltpu.VMEM((128, D), bf16),
        pltpu.VMEM((NY, OWN, F), f32),
        pltpu.VMEM((NY, OWN, 128), f32),
        pltpu.VMEM((2, 4, OWN, F), bf16),
        pltpu.VMEM((2, 4, OWN, F), bf16),
        pltpu.VMEM((2, 4, 16, 128), bf16),
        pltpu.VMEM((2, 4, 16, 128), bf16),
        pltpu.VMEM((NY, OWN, F), bf16),
        pltpu.VMEM((NY, 16, 128), bf16),
        pltpu.VMEM((NY, 16, 128), bf16),
        pltpu.VMEM((NY, 4, 16, R), f32),
        pltpu.VMEM((4, 8, 128), f32),
        pltpu.VMEM((R, OWN), f32),
        pltpu.VMEM((R, OWN), f32),
        pltpu.VMEM((NZ, 8, OWN), f32),
        pltpu.VMEM((NZ - 1, 8, OWN), f32),
        pltpu.VMEM((8, OWN), f32),
        pltpu.VMEM((NY - 1, 8, OWN), f32),
        pltpu.VMEM((NY, PD, OWN), f32),
        pltpu.VMEM((R, 512), bf16),
        pltpu.VMEM((NX, 16, F), f32),
        pltpu.VMEM((NX, 16, F), bf16),
        pltpu.VMEM((NX - 1, 16, F), bf16),
        pltpu.VMEM((16, F), bf16),
        pltpu.VMEM((NX - 1, 16, F), bf16),
        pltpu.VMEM((NX, 4, D), f32),
    ]
    for g in GROUPS:
        scratch += group_scratch(64 * len(g))
    scratch += [
        dma((7,)),
        dma((5, 7)), dma((5, 7)),
        dma((5,)), dma((5,)),
        dma((2, 4, Q)), dma((2, 4, Q)),
        dma((2, 4, Q)), dma((2, 4, Q)),
        dma((2, 4)), dma((2, 4)),
        dma((2, 4)), dma((2, 4)),
        dma, dma,
        dma((4,)), dma((4,)),
        dma((4, 7)), dma((4, 7)),
        dma, dma,
        dma((7,)), dma((7,)),
        dma((7,)), dma((7,)),
        dma((3, Q)), dma((3, Q)),
        dma((3, Q)), dma((3, Q)),
        dma((3,)), dma((3,)),
    ]
    shapes = (((PD, 512), bf16), ((4, D), f32), ((R, F), f32))
    parts = pl.pallas_call(
        kernel,
        out_shape=tuple(pltpu.VMEM(*s) for s in shapes),
        in_specs=[hbm] * 7,
        out_specs=(vmem,) * 3,
        scratch_shapes=scratch,
        compiler_params=pltpu.CompilerParams(
            collective_id=0, has_side_effects=True, vmem_limit_bytes=56 << 20
        ),
    )(tokens.T, codes, scales, down.T, up, up_branch, hidden_grad)
    out_t, gd_t, gu = pl.pallas_call(
        finish,
        out_shape=tuple(jax.ShapeDtypeStruct(*s) for s in shapes),
        in_specs=[hbm] * 3,
        out_specs=(hbm,) * 3,
        scratch_shapes=[dma((3,))],
    )(*(pltpu.with_memory_space_constraint(a, pltpu.VMEM) for a in parts))
    return out_t.T, gd_t.T, gu


def solution(mesh):
    return jax.shard_map(
        per_device,
        mesh=mesh,
        in_specs=(
            P("dp", ("row", "col")),
            P("row", "col"),
            P("row", "col"),
            P("row", None),
            P(None, "col"),
            P(("dp", "row"), "col"),
            P(("dp", "row"), "col"),
        ),
        out_specs=(P("dp", ("row", "col")), P("row", "col"), P(None, "col")),
        check_vma=False,
    )
```

```python
import jax
import jax.numpy as jnp
from jax import lax
from jax.experimental import pallas as pl
from jax.experimental.pallas import tpu as pltpu
from jax.sharding import PartitionSpec as P

MESH = pl.DeviceIdType.MESH
NX, NY, NZ = 4, 8, 8
OWN = 64
PD = 64
D = NZ * 2 * PD
F = 1664
R = 64
CHUNKS = ((0, 256), (256, 768), (768, 1280), (1280, 1536), (1536, 1664))
Q = len(CHUNKS)
RS_ORDER = (4, 0, 1, 2, 3)
TWO = 3
SPLIT = CHUNKS[TWO][0]
GROUPS = ((0, 1, 7), (2, 6), (3, 5), (4,))
PEERS = (4, 3, 5, 2, 6, 1, 7)
f32 = jnp.float32
bf16 = jnp.bfloat16
NT = (((1,), (1,)), ((), ()))


def block_of(rel):
    if rel in (4, 0):
        return 0, 0 if rel == 4 else 1
    return (4 - rel, 0) if rel < 4 else (rel - 4, 1)


def kernel(
    tok_hbm, codes_hbm, scale_hbm, down_hbm, up_hbm, ub_hbm, hg_hbm,
    out_ref, gd_ref, gu_ref,
    tok_ref, codes, scale_ref, down_ref, up_ref, ub, hg, scale, W, WA, G, PK, xt, part, part_a,
    rs_snd, rs_rcv, a_snd, a_rcv, GR, GA, GB, a_all, back, bk_snd, bk_rcv, bz_snd, bz_rcv, by_snd, by_rcv, zfin,
    at_ref, up_acc, up_all, xs_snd, xs_rcv, xg_snd, xg_rcv, gd_all,
    *rest,
):
    group_bufs, sems = rest[: 4 * 6], rest[4 * 6 :]
    (loc_sem, tok_s, tok_r, sib_s, sib_r, rs_s, rs_r, ag_s, ag_r,
     ra_s, ra_r, ga_s, ga_r, ab_s, ab_r,
     p_s, p_r, z_s, z_r, bp_s, bp_r, bz_s, bz_r, by_s, by_r, xs_s, xs_r, xg_s, xg_r, gd_s, gd_r) = sems
    x = lax.axis_index("dp")
    y = lax.axis_index("row")
    col = lax.axis_index("col")
    z = col // 2
    c = lax.rem(col, 2)
    sib = {"col": 2 * z + 1 - c}

    def yid(k):
        return {"row": lax.rem(y + k + NY, NY)}

    def zid(k):
        return {"col": 2 * lax.rem(z + k, NZ) + c}

    def xid(k):
        return {"dp": lax.rem(x + k, NX)}

    def owner(rel):
        return lax.rem(y + rel, NY)

    sent = []

    def drain(keep=0):
        done = sent[: len(sent) - keep]
        del sent[: len(done)]
        for cp in done:
            cp.wait_send()

    def send(src, dst, ss, rs, dev):
        cp = pltpu.make_async_remote_copy(
            src_ref=src, dst_ref=dst, send_sem=ss, recv_sem=rs, device_id=dev, device_id_type=MESH
        )
        cp.start()
        sent.append(cp)
        return cp

    loads = [
        pltpu.make_async_copy(src, dst, loc_sem.at[i])
        for i, (src, dst) in enumerate((
            (tok_hbm, tok_ref), (down_hbm, down_ref), (up_hbm, up_ref), (scale_hbm, scale_ref),
            (codes_hbm, codes), (ub_hbm, ub), (hg_hbm, hg),
        ))
    ]
    barrier = pltpu.get_barrier_semaphore()
    greet = [zid(k) for k in PEERS] + [yid(k) for k in PEERS] + [xid(k) for k in (2, 1, 3)] + [sib]
    for dev in greet:
        pl.semaphore_signal(barrier, inc=1, device_id=dev, device_id_type=MESH)
    for ld in loads:
        ld.start()
    loads[0].wait()

    def piece(rel):
        o = owner(rel)
        two = tok_ref[:, pl.ds(pl.multiple_of((o // 2) * 128, 128), 128)].astype(f32)
        return jnp.where(lax.rem(o, 2) == 1, two[:, 64:], two[:, :64])

    for j, rel in ((0, 4), (1, 0)):
        p = piece(rel)
        PK[j, z, c] = jnp.concatenate([p[:32], p[32:]], axis=1).astype(bf16)
    for b in (1, 2, 3):
        G[b, z, c] = jnp.concatenate([piece(4 - b), piece(4 + b)], axis=1).astype(bf16)
    pl.semaphore_wait(barrier, len(greet))

    def tokens_of(item):
        return PK.at[item // 4] if item in (0, 4) else G.at[item]

    tok = {}

    def spread(item):
        ref = tokens_of(item).at[z, c]
        for k in PEERS:
            tok[item, k] = send(ref, ref, tok_s.at[item, k - 1], tok_r.at[item, k - 1], zid(k))

    spread(0)

    for ld in loads[1:5]:
        ld.wait()
    scale[...] = scale_ref[...].astype(f32)

    def weight_block(i):
        rows = pl.ds(pl.multiple_of(i * 128, 128), 128)
        dn = down_ref[:, rows].astype(f32).T
        dn2 = (2.0 * dn).astype(bf16)
        for lo, hi in ((0, 512), (512, 1024), (1024, 1664)):
            low = jnp.dot(dn2, up_ref[:, lo:hi], preferred_element_type=f32)
            w = codes[rows, lo:hi].astype(f32) * scale[pl.ds(i, 1), lo:hi] + low
            W[i, :, :, lo:hi] = w.astype(bf16).reshape(2, PD, hi - lo)
        WA[i] = jnp.concatenate([dn, jnp.zeros_like(dn)], axis=1).astype(bf16).reshape(2, PD, 128)

    pl.loop(0, NZ // 2)(weight_block)
    spread(1)
    pl.loop(NZ // 2, NZ)(weight_block)
    for item in (2, 3, 4):
        spread(item)

    fwd = {}

    def forward(item):
        for k in PEERS:
            tok[item, k].wait_recv()
        ref = tokens_of(item).at[:, c]
        fwd[item] = send(ref, ref, sib_s.at[item], sib_r.at[item], sib)

    def landed(item):
        fwd[item].wait_recv()
        if item in (0, 4):
            xt[:, :512] = PK[item // 4].reshape(512, 128).T
        else:
            xt[...] = G[item].reshape(D, 128).T

    def times(item, w, lo, hi):
        if item in (0, 4):
            return jnp.dot(
                xt[:64, :512], w[:, :, :32, lo:hi].reshape(512, hi - lo), preferred_element_type=f32
            ) + jnp.dot(
                xt[64:, :512], w[:, :, 32:, lo:hi].reshape(512, hi - lo), preferred_element_type=f32
            )
        return jnp.dot(xt[...], w[:, :, :, lo:hi].reshape(D, hi - lo), preferred_element_type=f32)

    def rels(item):
        return (4 - item,) if item in (0, 4) else (4 - item, 4 + item)

    def gemm1(item, q):
        lo, hi = CHUNKS[q]
        p = times(item, W, lo, hi)
        for i, rel in enumerate(rels(item)):
            part[rel, :, lo:hi] = p[64 * i : 64 * i + 64]

    def gemm_a(item):
        p = times(item, WA, 0, 128)
        for i, rel in enumerate(rels(item)):
            part_a[rel] = p[64 * i : 64 * i + 64]

    def packed(rel):
        v = part_a[rel, pl.ds(pl.multiple_of(c * 32, 32), 32), :]
        return v[:16] + jnp.concatenate([v[16:, 64:], v[16:, :64]], axis=1)

    rs = {}

    def rs_step(step, q):
        lo, hi = CHUNKS[q]
        for d, sign in ((0, 1), (1, -1)):
            rel = (sign * (5 - step)) % 8
            half = slice(0, 32) if d == 0 else slice(32, 64)
            other = slice(32, 64) if d == 0 else slice(0, 32)
            dst = rs_snd.at[d, step - 1]
            if step == 1:
                rs_snd[d, 0, half, lo:hi] = part[rel, half, lo:hi].astype(bf16)
                src, tgt = dst.at[half, lo:hi], rs_rcv.at[d, 0, half, lo:hi]
            else:
                rs[d, step - 1, q].wait_recv()
                if step == 2:
                    rs_snd[d, 1, half, lo:hi] = (
                        part[rel, half, lo:hi] + rs_rcv[d, 0, half, lo:hi].astype(f32)
                    ).astype(bf16)
                    rs_snd[d, 1, other, lo:hi] = part[rel, other, lo:hi].astype(bf16)
                else:
                    rs_snd[d, step - 1, :, lo:hi] = (
                        part[rel, :, lo:hi] + rs_rcv[d, step - 2, :, lo:hi].astype(f32)
                    ).astype(bf16)
                src, tgt = dst.at[:, lo:hi], rs_rcv.at[d, step - 1, :, lo:hi]
            rs[d, step, q] = send(
                src, tgt, rs_s.at[d, step - 1, q], rs_r.at[d, step - 1, q], yid(sign)
            )

    ra = {}

    def rs_a(step):
        for d, sign in ((0, 1), (1, -1)):
            if d == 1 and step == 1:
                continue
            v = packed((sign * (5 - step)) % 8)
            if step > 1 + d:
                ra[d, step - 1].wait_recv()
                v = v + a_rcv[d, step - 2].astype(f32)
            a_snd[d, step - 1] = v.astype(bf16)
            ra[d, step] = send(
                a_snd.at[d, step - 1], a_rcv.at[d, step - 1],
                ra_s.at[d, step - 1], ra_r.at[d, step - 1], yid(sign),
            )

    def sum_a():
        ra[0, 4].wait_recv()
        ra[1, 4].wait_recv()
        GA[y] = (packed(0) + a_rcv[0, 3].astype(f32) + a_rcv[1, 3].astype(f32)).astype(bf16)

    ga = {}

    def ag_a(hop):
        for d, sign in ((0, 1), (1, -1)):
            if hop > 1:
                ga[d, hop - 1].wait_recv()
            if d == 1 and hop == 4:
                continue
            ref = GA.at[owner((-sign * (hop - 1)) % 8)]
            ga[d, hop] = send(ref, ref, ga_s.at[d, hop - 1], ga_r.at[d, hop - 1], yid(sign))

    def gating(q):
        lo, hi = CHUNKS[q]
        rs[0, 4, q].wait_recv()
        rs[1, 4, q].wait_recv()
        total = part[0, :, lo:hi] + rs_rcv[0, 3, :, lo:hi].astype(f32) + rs_rcv[1, 3, :, lo:hi].astype(f32)
        s = jax.nn.sigmoid(total)
        product = hg[:, lo:hi].astype(f32) * ub[:, lo:hi].astype(f32)
        GR[y, :, lo:hi] = (product * s * (1.0 + total * (1.0 - s))).astype(bf16)

    ag = {}

    def ag_hop(hop, q):
        lo, hi = CHUNKS[q]
        for d, sign in ((0, 1), (1, -1)):
            if hop > 1:
                ag[d, hop - 1, q].wait_recv()
            o = owner((-sign * (hop - 1)) % 8)
            rows = slice(0, 64)
            if hop == 4:
                rows = slice(0, 32) if d == 0 else slice(32, 64)
            ref = GR.at[o, rows, lo:hi]
            ag[d, hop, q] = send(ref, ref, ag_s.at[d, hop - 1, q], ag_r.at[d, hop - 1, q], yid(sign))

    bp, zb, yb = [], {}, {}

    def back_own():
        bk = lax.dot_general(up_ref[...], GR[y], NT, preferred_element_type=f32)
        bk_snd[...] = 2.0 * bk
        bp.append(send(bk_snd, bk_rcv, bp_s, bp_r, sib))

    def back_z():
        bp[0].wait_recv()
        bz_snd[...] = (bk_snd[...] + bk_rcv[...]).reshape(NZ, 8, OWN)
        for k in PEERS:
            zb[k] = send(
                bz_snd.at[lax.rem(z + k, NZ)], bz_rcv.at[k - 1], bz_s.at[k - 1], bz_r.at[k - 1], zid(k)
            )

    def back_y():
        total = bz_snd[z]
        for k in PEERS:
            zb[k].wait_recv()
            total = total + bz_rcv[k - 1]
        by_snd[...] = total
        for k in PEERS:
            yb[k] = send(by_snd, by_rcv.at[k - 1], by_s.at[k - 1], by_r.at[k - 1], yid(k))

    def back_end():
        for k in (0,) + PEERS:
            if k:
                yb[k].wait_recv()
            b, h = block_of((8 - k) % 8)
            back[b, :, h * 64 : h * 64 + 64] = by_rcv[k - 1] if k else by_snd[...]

    pair, zs = {}, {}

    def bufs(g):
        return group_bufs[6 * g : 6 * g + 6]

    def group_add(g, q):
        lo, hi = CHUNKS[q]
        n = 64 * len(GROUPS[g])
        gr = jnp.concatenate([GR[owner(rel), :, lo:hi] for rel in GROUPS[g]], axis=0)
        for ref, core in zip(bufs(g)[4:], (1 - c, c)):
            term = lax.dot_general(
                W[:, core, :, lo:hi].reshape(512, hi - lo), gr, NT, preferred_element_type=f32
            ).reshape(NZ, PD, n)
            ref[...] = term if q == 0 else ref[...] + term

    def compact(g, v):
        return jnp.concatenate([v[:, :32], v[:, 32:]], axis=2) if g == 3 else v

    def group_pair(g):
        psnd, prcv = bufs(g)[:2]
        psnd[...] = compact(g, bufs(g)[4][...]).astype(bf16)
        pair[g] = send(psnd, prcv, p_s.at[g], p_r.at[g], sib)

    def group_own(g):
        _, prcv, zsnd, zrcv, _, own = bufs(g)
        pair[g].wait_recv()
        zsnd[...] = (compact(g, own[...]) + prcv[...].astype(f32)).astype(bf16)
        for k in PEERS:
            zs[g, k] = send(
                zsnd.at[lax.rem(z + k, NZ)], zrcv.at[k - 1], z_s.at[g, k - 1], z_r.at[g, k - 1], zid(k)
            )

    def group_end(g):
        zsnd, zrcv = bufs(g)[2:4]
        total = zsnd[z].astype(f32)
        for k in PEERS:
            zs[g, k].wait_recv()
            total = total + zrcv[k - 1].astype(f32)
        if g == 3:
            zfin[4, :32] = total[:, :64]
            zfin[4, 32:] = total[:, 64:]
            return
        for i, rel in enumerate(GROUPS[g]):
            zfin[rel] = total[:, i * 64 : i * 64 + 64]

    gds = []

    def down_grad():
        back_end()
        gd = jnp.zeros((8, D), f32)
        for b in range(4):
            gd = gd + lax.dot_general(
                back[b].astype(bf16), G[b].reshape(D, 128), NT, preferred_element_type=f32
            )
        gd_all[x] = jnp.where(c == 0, gd[:4], gd[4:]) * (1.0 / 2048.0)
        for k in (2, 1, 3):
            gds.append(send(gd_all.at[x], gd_all.at[x], gd_s.at[k - 1], gd_r.at[k - 1], xid(k)))

    forward(0)
    landed(0)
    for i, q in enumerate(RS_ORDER):
        gemm1(0, q)
        rs_step(1, q)
        if i == 1:
            gemm_a(0)
            rs_a(1)
    for step in (2, 3, 4):
        if step == 2:
            forward(1)
        landed(step - 1)
        for q in RS_ORDER:
            gemm1(step - 1, q)
        gemm_a(step - 1)
        forward(step)
        for i, q in enumerate(RS_ORDER):
            rs_step(step, q)
            if i == 1:
                rs_a(step)
    landed(4)
    for q in RS_ORDER:
        gemm1(4, q)
    gemm_a(4)
    loads[5].wait()
    loads[6].wait()

    gating(4)
    for q in range(Q):
        if q < 4:
            gating(q)
        ag_hop(1, q)
        if q == 0:
            sum_a()
            ag_a(1)
    back_own()
    drain(19)
    low, high = [
        jnp.concatenate([PK[0, :, :, :, h].astype(f32), PK[1, :, :, :, h].astype(f32)], axis=3).astype(bf16)
        for h in (slice(0, 64), slice(64, 128))
    ]
    G[0, :, :, :32, :] = low
    G[0, :, :, 32:, :] = high
    for hop, g in ((2, 0), (3, 1), (4, 2)):
        for q in range(Q):
            ag_hop(hop, q)
            if q == 0:
                ag_a(hop)
            group_add(g, q)
            if g > 0 and q == 0:
                group_own(g - 1)
            if g == 0 and q == 1:
                back_z()
            if g == 1 and q == 2:
                back_y()
            if g == 2 and q == 3:
                down_grad()
        group_pair(g)

    xs, xg = {}, {}

    def last(q):
        ag[0, 4, q].wait_recv()
        ag[1, 4, q].wait_recv()

    def up_part(q):
        lo, hi = CHUNKS[q]
        u = jnp.dot(at_ref[...], GR[:, :, lo:hi].reshape(512, hi - lo), preferred_element_type=f32)
        u = u * (2.0 / 2048.0)
        if q >= TWO:
            up_all[x, :, lo - SPLIT : hi - SPLIT] = u.astype(bf16)
            ref = up_all.at[x, :, lo - SPLIT : hi - SPLIT]
            for k in (2, 1, 3):
                xs[k, q] = send(ref, ref, xs_s.at[k - 1, q], xs_r.at[k - 1, q], xid(k))
            return
        u = u.reshape(NX, 16, hi - lo)
        up_acc[:, :, lo:hi] = u
        xs_snd[:, :, lo:hi] = u.astype(bf16)
        for k in (2, 1, 3):
            xs[k, q] = send(
                xs_snd.at[lax.rem(x + k, NX), :, lo:hi], xs_rcv.at[k - 1, :, lo:hi],
                xs_s.at[k - 1, q], xs_r.at[k - 1, q], xid(k),
            )

    def up_sum(q):
        lo, hi = CHUNKS[q]
        total = up_acc[x, :, lo:hi]
        for k in (1, 2, 3):
            xs[k, q].wait_recv()
            total = total + xs_rcv[k - 1, :, lo:hi].astype(f32)
        xg_snd[:, lo:hi] = total.astype(bf16)
        for k in (2, 1, 3):
            xg[k, q] = send(
                xg_snd.at[:, lo:hi], xg_rcv.at[k - 1, :, lo:hi],
                xg_s.at[k - 1, q], xg_r.at[k - 1, q], xid(k),
            )

    ga[0, 4].wait_recv()
    swap = send(GA, GB, ab_s, ab_r, sib)
    last(0)
    group_add(3, 0)
    group_own(2)
    swap.wait_recv()
    for half, src in ((c, GA), (1 - c, GB)):
        v = src[...].astype(f32)
        a_all[:, 2 * half] = v[:, :, :64]
        a_all[:, 2 * half + 1] = v[:, :, 64:]
    at_ref[...] = a_all[...].reshape(512, R).T.astype(bf16)
    up_part(0)
    for q in range(1, Q):
        last(q)
        group_add(3, q)
        if q < Q - 1:
            up_part(q)
    group_pair(3)
    up_part(Q - 1)
    group_own(3)

    for q in range(TWO):
        up_sum(q)
    group_end(0)
    group_end(1)

    group_end(2)
    drain(24)
    group_end(3)
    for i in range(4):
        a = zfin[lax.rem(2 * i - y + NY, NY)]
        b = zfin[lax.rem(2 * i + 1 - y + NY, NY)]
        out_ref[:, i * 128 : i * 128 + 128] = jnp.concatenate([a, b], axis=1).astype(bf16)

    for q in range(TWO, Q):
        for k in (1, 2, 3):
            xs[k, q].wait_recv()
    gu_ref[:, SPLIT:] = (
        up_all[0].astype(f32) + up_all[1].astype(f32) + up_all[2].astype(f32) + up_all[3].astype(f32)
    )
    for q in range(TWO):
        for k in (1, 2, 3):
            xg[k, q].wait_recv()
    gu_ref[pl.ds(pl.multiple_of(x * 16, 16), 16), :SPLIT] = xg_snd[...].astype(f32)
    for k in (1, 2, 3):
        at = pl.multiple_of(lax.rem(x - k + NX, NX) * 16, 16)
        gu_ref[pl.ds(at, 16), :SPLIT] = xg_rcv[k - 1].astype(f32)
    for cp in gds:
        cp.wait_recv()
    gd_ref[...] = gd_all[0] + gd_all[1] + gd_all[2] + gd_all[3]
    drain()


def finish(out_ref, gd_ref, gu_ref, out_hbm, gd_hbm, gu_hbm, sem):
    copies = [
        pltpu.make_async_copy(src, dst, sem.at[i])
        for i, (src, dst) in enumerate(((gu_ref, gu_hbm), (out_ref, out_hbm), (gd_ref, gd_hbm)))
    ]
    for cp in copies:
        cp.start()
    for cp in copies:
        cp.wait()


def group_scratch(n):
    d, t = (PD // 2, 128) if n == 64 else (PD, n)
    return [
        pltpu.VMEM((NZ, d, t), bf16),
        pltpu.VMEM((NZ, d, t), bf16),
        pltpu.VMEM((NZ, d, t), bf16),
        pltpu.VMEM((NZ - 1, d, t), bf16),
        pltpu.VMEM((NZ, PD, n), f32),
        pltpu.VMEM((NZ, PD, n), f32),
    ]


def per_device(tokens, codes, scales, down, up, up_branch, hidden_grad):
    vmem = pl.BlockSpec(memory_space=pltpu.VMEM)
    hbm = pl.BlockSpec(memory_space=pl.ANY)
    dma = pltpu.SemaphoreType.DMA
    scratch = [
        pltpu.VMEM((PD, 512), bf16),
        pltpu.VMEM((D, F), bf16),
        pltpu.VMEM((8, F), bf16),
        pltpu.VMEM((R, D), bf16),
        pltpu.VMEM((R, F), bf16),
        pltpu.VMEM((OWN, F), bf16),
        pltpu.VMEM((OWN, F), bf16),
        pltpu.VMEM((8, F), f32),
        pltpu.VMEM((NZ, 2, PD, F), bf16),
        pltpu.VMEM((NZ, 2, PD, 128), bf16),
        pltpu.VMEM((4, NZ, 2, PD, 128), bf16),
        pltpu.VMEM((2, NZ, 2, PD // 2, 128), bf16),
        pltpu.VMEM((128, D), bf16),
        pltpu.VMEM((NY, OWN, F), f32),
        pltpu.VMEM((NY, OWN, 128), f32),
        pltpu.VMEM((2, 4, OWN, F), bf16),
        pltpu.VMEM((2, 4, OWN, F), bf16),
        pltpu.VMEM((2, 4, 16, 128), bf16),
        pltpu.VMEM((2, 4, 16, 128), bf16),
        pltpu.VMEM((NY, OWN, F), bf16),
        pltpu.VMEM((NY, 16, 128), bf16),
        pltpu.VMEM((NY, 16, 128), bf16),
        pltpu.VMEM((NY, 4, 16, R), f32),
        pltpu.VMEM((4, 8, 128), f32),
        pltpu.VMEM((R, OWN), f32),
        pltpu.VMEM((R, OWN), f32),
        pltpu.VMEM((NZ, 8, OWN), f32),
        pltpu.VMEM((NZ - 1, 8, OWN), f32),
        pltpu.VMEM((8, OWN), f32),
        pltpu.VMEM((NY - 1, 8, OWN), f32),
        pltpu.VMEM((NY, PD, OWN), f32),
        pltpu.VMEM((R, 512), bf16),
        pltpu.VMEM((NX, 16, SPLIT), f32),
        pltpu.VMEM((NX, R, F - SPLIT), bf16),
        pltpu.VMEM((NX, 16, SPLIT), bf16),
        pltpu.VMEM((NX - 1, 16, SPLIT), bf16),
        pltpu.VMEM((16, SPLIT), bf16),
        pltpu.VMEM((NX - 1, 16, SPLIT), bf16),
        pltpu.VMEM((NX, 4, D), f32),
    ]
    for g in GROUPS:
        scratch += group_scratch(64 * len(g))
    scratch += [
        dma((7,)),
        dma((5, 7)), dma((5, 7)),
        dma((5,)), dma((5,)),
        dma((2, 4, Q)), dma((2, 4, Q)),
        dma((2, 4, Q)), dma((2, 4, Q)),
        dma((2, 4)), dma((2, 4)),
        dma((2, 4)), dma((2, 4)),
        dma, dma,
        dma((4,)), dma((4,)),
        dma((4, 7)), dma((4, 7)),
        dma, dma,
        dma((7,)), dma((7,)),
        dma((7,)), dma((7,)),
        dma((3, Q)), dma((3, Q)),
        dma((3, Q)), dma((3, Q)),
        dma((3,)), dma((3,)),
    ]
    shapes = (((PD, 512), bf16), ((4, D), f32), ((R, F), f32))
    parts = pl.pallas_call(
        kernel,
        out_shape=tuple(pltpu.VMEM(*s) for s in shapes),
        in_specs=[hbm] * 7,
        out_specs=(vmem,) * 3,
        scratch_shapes=scratch,
        compiler_params=pltpu.CompilerParams(
            collective_id=0, has_side_effects=True, vmem_limit_bytes=56 << 20
        ),
    )(tokens.T, codes, scales, down.T, up, up_branch, hidden_grad)
    out_t, gd_t, gu = pl.pallas_call(
        finish,
        out_shape=tuple(jax.ShapeDtypeStruct(*s) for s in shapes),
        in_specs=[hbm] * 3,
        out_specs=(hbm,) * 3,
        scratch_shapes=[dma((3,))],
    )(*(pltpu.with_memory_space_constraint(a, pltpu.VMEM) for a in parts))
    return out_t.T, gd_t.T, gu


def solution(mesh):
    return jax.shard_map(
        per_device,
        mesh=mesh,
        in_specs=(
            P("dp", ("row", "col")),
            P("row", "col"),
            P("row", "col"),
            P("row", None),
            P(None, "col"),
            P(("dp", "row"), "col"),
            P(("dp", "row"), "col"),
        ),
        out_specs=(P("dp", ("row", "col")), P("row", "col"), P(None, "col")),
        check_vma=False,
    )
```

```python
import jax
import jax.numpy as jnp
from jax import lax
from jax.experimental import pallas as pl
from jax.experimental.pallas import tpu as pltpu
from jax.sharding import PartitionSpec as P

MESH = pl.DeviceIdType.MESH
NX, NY, NZ = 4, 8, 8
OWN = 64
PD = 64
D = NZ * 2 * PD
F = 1664
R = 64
CHUNKS = ((0, 256), (256, 768), (768, 1280), (1280, 1536), (1536, 1664))
Q = len(CHUNKS)
RS_ORDER = (4, 0, 1, 2, 3)
TWO = 3
SPLIT = CHUNKS[TWO][0]
GROUPS = ((0, 1, 7), (2, 6), (3, 5), (4,))
PEERS = (4, 3, 5, 2, 6, 1, 7)
f32 = jnp.float32
bf16 = jnp.bfloat16
NT = (((1,), (1,)), ((), ()))


def block_of(rel):
    if rel in (4, 0):
        return 0, 0 if rel == 4 else 1
    return (4 - rel, 0) if rel < 4 else (rel - 4, 1)


def kernel(
    tok_hbm, codes_hbm, scale_hbm, down_hbm, up_hbm, ub_hbm, hg_hbm,
    out_ref, gd_ref, gu_ref,
    tok_ref, codes, scale_ref, down_ref, up_ref, ub, hg, scale, W, WA, G, PK, xt, part, part_a,
    rs_snd, rs_rcv, a_snd, a_rcv, GR, GA, GB, a_all, back, bk_snd, bk_rcv, bz_snd, bz_rcv, by_snd, by_rcv, zfin,
    at_ref, up_acc, up_all, xs_snd, xs_rcv, xg_snd, xg_rcv, gd_all,
    *rest,
):
    group_bufs, sems = rest[: 4 * 6], rest[4 * 6 :]
    (loc_sem, tok_s, tok_r, sib_s, sib_r, rs_s, rs_r, ag_s, ag_r,
     ra_s, ra_r, ga_s, ga_r, ab_s, ab_r,
     p_s, p_r, z_s, z_r, bp_s, bp_r, bz_s, bz_r, by_s, by_r, xs_s, xs_r, xg_s, xg_r, gd_s, gd_r) = sems
    x = lax.axis_index("dp")
    y = lax.axis_index("row")
    col = lax.axis_index("col")
    z = col // 2
    c = lax.rem(col, 2)
    sib = {"col": 2 * z + 1 - c}

    def yid(k):
        return {"row": lax.rem(y + k + NY, NY)}

    def zid(k):
        return {"col": 2 * lax.rem(z + k, NZ) + c}

    def xid(k):
        return {"dp": lax.rem(x + k, NX)}

    def owner(rel):
        return lax.rem(y + rel, NY)

    sent = []

    def drain(keep=0):
        done = sent[: len(sent) - keep]
        del sent[: len(done)]
        for cp in done:
            cp.wait_send()

    def send(src, dst, ss, rs, dev):
        cp = pltpu.make_async_remote_copy(
            src_ref=src, dst_ref=dst, send_sem=ss, recv_sem=rs, device_id=dev, device_id_type=MESH
        )
        cp.start()
        sent.append(cp)
        return cp

    loads = [
        pltpu.make_async_copy(src, dst, loc_sem.at[i])
        for i, (src, dst) in enumerate((
            (tok_hbm, tok_ref), (down_hbm, down_ref), (up_hbm, up_ref), (scale_hbm, scale_ref),
            (codes_hbm, codes), (ub_hbm, ub), (hg_hbm, hg),
        ))
    ]
    barrier = pltpu.get_barrier_semaphore()
    greet = [zid(k) for k in PEERS] + [yid(k) for k in PEERS] + [xid(k) for k in (2, 1, 3)] + [sib]
    for dev in greet:
        pl.semaphore_signal(barrier, inc=1, device_id=dev, device_id_type=MESH)
    for ld in loads:
        ld.start()
    loads[0].wait()

    def piece(rel):
        o = owner(rel)
        two = tok_ref[:, pl.ds(pl.multiple_of((o // 2) * 128, 128), 128)].astype(f32)
        return jnp.where(lax.rem(o, 2) == 1, two[:, 64:], two[:, :64])

    for j, rel in ((0, 4), (1, 0)):
        p = piece(rel)
        PK[j, z, c] = jnp.concatenate([p[:32], p[32:]], axis=1).astype(bf16)
    for b in (1, 2, 3):
        G[b, z, c] = jnp.concatenate([piece(4 - b), piece(4 + b)], axis=1).astype(bf16)
    pl.semaphore_wait(barrier, len(greet))

    def tokens_of(item):
        return PK.at[item // 4] if item in (0, 4) else G.at[item]

    tok = {}

    def spread(item):
        ref = tokens_of(item).at[z, c]
        for k in PEERS:
            tok[item, k] = send(ref, ref, tok_s.at[item, k - 1], tok_r.at[item, k - 1], zid(k))

    spread(0)

    for ld in loads[1:5]:
        ld.wait()
    scale[...] = scale_ref[...].astype(f32)

    def weight_block(i):
        rows = pl.ds(pl.multiple_of(i * 128, 128), 128)
        dn = down_ref[:, rows].astype(f32).T
        dn2 = (2.0 * dn).astype(bf16)
        for lo, hi in ((0, 512), (512, 1024), (1024, 1664)):
            low = jnp.dot(dn2, up_ref[:, lo:hi], preferred_element_type=f32)
            w = codes[rows, lo:hi].astype(f32) * scale[pl.ds(i, 1), lo:hi] + low
            W[i, :, :, lo:hi] = w.astype(bf16).reshape(2, PD, hi - lo)
        WA[i] = jnp.concatenate([dn, jnp.zeros_like(dn)], axis=1).astype(bf16).reshape(2, PD, 128)

    pl.loop(0, NZ // 2)(weight_block)
    spread(1)
    pl.loop(NZ // 2, NZ)(weight_block)
    for item in (2, 3, 4):
        spread(item)

    fwd = {}

    def forward(item):
        for k in PEERS:
            tok[item, k].wait_recv()
        ref = tokens_of(item).at[:, c]
        fwd[item] = send(ref, ref, sib_s.at[item], sib_r.at[item], sib)

    def landed(item):
        fwd[item].wait_recv()
        if item in (0, 4):
            xt[:, :512] = PK[item // 4].reshape(512, 128).T
        else:
            xt[...] = G[item].reshape(D, 128).T

    def times(item, w, lo, hi):
        if item in (0, 4):
            return jnp.dot(
                xt[:64, :512], w[:, :, :32, lo:hi].reshape(512, hi - lo), preferred_element_type=f32
            ) + jnp.dot(
                xt[64:, :512], w[:, :, 32:, lo:hi].reshape(512, hi - lo), preferred_element_type=f32
            )
        return jnp.dot(xt[...], w[:, :, :, lo:hi].reshape(D, hi - lo), preferred_element_type=f32)

    def rels(item):
        return (4 - item,) if item in (0, 4) else (4 - item, 4 + item)

    def gemm1(item, q):
        lo, hi = CHUNKS[q]
        p = times(item, W, lo, hi)
        for i, rel in enumerate(rels(item)):
            part[rel, :, lo:hi] = p[64 * i : 64 * i + 64]

    def gemm_a(item):
        p = times(item, WA, 0, 128)
        for i, rel in enumerate(rels(item)):
            part_a[rel] = p[64 * i : 64 * i + 64]

    def packed(rel):
        v = part_a[rel, pl.ds(pl.multiple_of(c * 32, 32), 32), :]
        return v[:16] + jnp.concatenate([v[16:, 64:], v[16:, :64]], axis=1)

    rs = {}

    def rs_step(step, q):
        lo, hi = CHUNKS[q]
        for d, sign in ((0, 1), (1, -1)):
            rel = (sign * (5 - step)) % 8
            half = slice(0, 32) if d == 0 else slice(32, 64)
            other = slice(32, 64) if d == 0 else slice(0, 32)
            dst = rs_snd.at[d, step - 1]
            if step == 1:
                rs_snd[d, 0, half, lo:hi] = part[rel, half, lo:hi].astype(bf16)
                src, tgt = dst.at[half, lo:hi], rs_rcv.at[d, 0, half, lo:hi]
            else:
                rs[d, step - 1, q].wait_recv()
                if step == 2:
                    rs_snd[d, 1, half, lo:hi] = (
                        part[rel, half, lo:hi] + rs_rcv[d, 0, half, lo:hi].astype(f32)
                    ).astype(bf16)
                    rs_snd[d, 1, other, lo:hi] = part[rel, other, lo:hi].astype(bf16)
                else:
                    rs_snd[d, step - 1, :, lo:hi] = (
                        part[rel, :, lo:hi] + rs_rcv[d, step - 2, :, lo:hi].astype(f32)
                    ).astype(bf16)
                src, tgt = dst.at[:, lo:hi], rs_rcv.at[d, step - 1, :, lo:hi]
            rs[d, step, q] = send(
                src, tgt, rs_s.at[d, step - 1, q], rs_r.at[d, step - 1, q], yid(sign)
            )

    ra = {}

    def rs_a(step):
        for d, sign in ((0, 1), (1, -1)):
            if d == 1 and step == 1:
                continue
            v = packed((sign * (5 - step)) % 8)
            if step > 1 + d:
                ra[d, step - 1].wait_recv()
                v = v + a_rcv[d, step - 2].astype(f32)
            a_snd[d, step - 1] = v.astype(bf16)
            ra[d, step] = send(
                a_snd.at[d, step - 1], a_rcv.at[d, step - 1],
                ra_s.at[d, step - 1], ra_r.at[d, step - 1], yid(sign),
            )

    def sum_a():
        ra[0, 4].wait_recv()
        ra[1, 4].wait_recv()
        GA[y] = (packed(0) + a_rcv[0, 3].astype(f32) + a_rcv[1, 3].astype(f32)).astype(bf16)

    ga = {}

    def ag_a(hop):
        for d, sign in ((0, 1), (1, -1)):
            if hop > 1:
                ga[d, hop - 1].wait_recv()
            if d == 1 and hop == 4:
                continue
            ref = GA.at[owner((-sign * (hop - 1)) % 8)]
            ga[d, hop] = send(ref, ref, ga_s.at[d, hop - 1], ga_r.at[d, hop - 1], yid(sign))

    def gating(q):
        lo, hi = CHUNKS[q]
        rs[0, 4, q].wait_recv()
        rs[1, 4, q].wait_recv()
        total = part[0, :, lo:hi] + rs_rcv[0, 3, :, lo:hi].astype(f32) + rs_rcv[1, 3, :, lo:hi].astype(f32)
        s = jax.nn.sigmoid(total)
        product = hg[:, lo:hi].astype(f32) * ub[:, lo:hi].astype(f32)
        GR[y, :, lo:hi] = (product * s * (1.0 + total * (1.0 - s))).astype(bf16)

    ag = {}

    def ag_hop(hop, q):
        lo, hi = CHUNKS[q]
        for d, sign in ((0, 1), (1, -1)):
            if hop > 1:
                ag[d, hop - 1, q].wait_recv()
            o = owner((-sign * (hop - 1)) % 8)
            rows = slice(0, 64)
            if hop == 4:
                rows = slice(0, 32) if d == 0 else slice(32, 64)
            ref = GR.at[o, rows, lo:hi]
            ag[d, hop, q] = send(ref, ref, ag_s.at[d, hop - 1, q], ag_r.at[d, hop - 1, q], yid(sign))

    bp, zb, yb = [], {}, {}

    def back_own():
        bk = lax.dot_general(up_ref[...], GR[y], NT, preferred_element_type=f32)
        bk_snd[...] = 2.0 * bk
        bp.append(send(bk_snd, bk_rcv, bp_s, bp_r, sib))

    def back_z():
        bp[0].wait_recv()
        bz_snd[...] = (bk_snd[...] + bk_rcv[...]).reshape(NZ, 8, OWN)
        for k in PEERS:
            zb[k] = send(
                bz_snd.at[lax.rem(z + k, NZ)], bz_rcv.at[k - 1], bz_s.at[k - 1], bz_r.at[k - 1], zid(k)
            )

    def back_y():
        total = bz_snd[z]
        for k in PEERS:
            zb[k].wait_recv()
            total = total + bz_rcv[k - 1]
        by_snd[...] = jnp.where(c == 0, total[:4], total[4:])
        for k in PEERS:
            yb[k] = send(by_snd, by_rcv.at[k - 1], by_s.at[k - 1], by_r.at[k - 1], yid(k))

    def back_end():
        for k in (0,) + PEERS:
            if k:
                yb[k].wait_recv()
            b, h = block_of((8 - k) % 8)
            back[b, :, h * 64 : h * 64 + 64] = by_rcv[k - 1] if k else by_snd[...]

    pair, zs = {}, {}

    def bufs(g):
        return group_bufs[6 * g : 6 * g + 6]

    def group_add(g, q):
        lo, hi = CHUNKS[q]
        n = 64 * len(GROUPS[g])
        gr = jnp.concatenate([GR[owner(rel), :, lo:hi] for rel in GROUPS[g]], axis=0)
        for ref, core in zip(bufs(g)[4:], (1 - c, c)):
            term = lax.dot_general(
                W[:, core, :, lo:hi].reshape(512, hi - lo), gr, NT, preferred_element_type=f32
            ).reshape(NZ, PD, n)
            ref[...] = term if q == 0 else ref[...] + term

    def compact(g, v):
        return jnp.concatenate([v[:, :32], v[:, 32:]], axis=2) if g == 3 else v

    def group_pair(g):
        psnd, prcv = bufs(g)[:2]
        psnd[...] = compact(g, bufs(g)[4][...]).astype(bf16)
        pair[g] = send(psnd, prcv, p_s.at[g], p_r.at[g], sib)

    def group_own(g):
        _, prcv, zsnd, zrcv, _, own = bufs(g)
        pair[g].wait_recv()
        zsnd[...] = (compact(g, own[...]) + prcv[...].astype(f32)).astype(bf16)
        for k in PEERS:
            zs[g, k] = send(
                zsnd.at[lax.rem(z + k, NZ)], zrcv.at[k - 1], z_s.at[g, k - 1], z_r.at[g, k - 1], zid(k)
            )

    def group_end(g):
        zsnd, zrcv = bufs(g)[2:4]
        total = zsnd[z].astype(f32)
        for k in PEERS:
            zs[g, k].wait_recv()
            total = total + zrcv[k - 1].astype(f32)
        if g == 3:
            zfin[4, :32] = total[:, :64]
            zfin[4, 32:] = total[:, 64:]
            return
        for i, rel in enumerate(GROUPS[g]):
            zfin[rel] = total[:, i * 64 : i * 64 + 64]

    gds = []

    def down_grad():
        back_end()
        gd = jnp.zeros((4, D), f32)
        for b in range(4):
            gd = gd + lax.dot_general(
                back[b].astype(bf16), G[b].reshape(D, 128), NT, preferred_element_type=f32
            )
        gd_all[x] = gd * (1.0 / 2048.0)
        for k in (2, 1, 3):
            gds.append(send(gd_all.at[x], gd_all.at[x], gd_s.at[k - 1], gd_r.at[k - 1], xid(k)))

    forward(0)
    landed(0)
    for i, q in enumerate(RS_ORDER):
        gemm1(0, q)
        rs_step(1, q)
        if i == 1:
            gemm_a(0)
            rs_a(1)
    for step in (2, 3, 4):
        if step == 2:
            forward(1)
        landed(step - 1)
        for q in RS_ORDER:
            gemm1(step - 1, q)
        gemm_a(step - 1)
        forward(step)
        for i, q in enumerate(RS_ORDER):
            rs_step(step, q)
            if i == 1:
                rs_a(step)
    landed(4)
    for q in RS_ORDER:
        gemm1(4, q)
    gemm_a(4)
    loads[5].wait()
    loads[6].wait()

    gating(4)
    for q in range(Q):
        if q < 4:
            gating(q)
        ag_hop(1, q)
        if q == 0:
            sum_a()
            ag_a(1)
    back_own()
    drain(19)
    low, high = [
        jnp.concatenate([PK[0, :, :, :, h].astype(f32), PK[1, :, :, :, h].astype(f32)], axis=3).astype(bf16)
        for h in (slice(0, 64), slice(64, 128))
    ]
    G[0, :, :, :32, :] = low
    G[0, :, :, 32:, :] = high
    for hop, g in ((2, 0), (3, 1), (4, 2)):
        for q in range(Q):
            ag_hop(hop, q)
            if q == 0:
                ag_a(hop)
            group_add(g, q)
            if g > 0 and q == 0:
                group_own(g - 1)
            if g == 0 and q == 1:
                back_z()
            if g == 1 and q == 2:
                back_y()
            if g == 2 and q == 3:
                down_grad()
        group_pair(g)

    xs, xg = {}, {}

    def last(q):
        ag[0, 4, q].wait_recv()
        ag[1, 4, q].wait_recv()

    def up_part(q):
        lo, hi = CHUNKS[q]
        u = jnp.dot(at_ref[...], GR[:, :, lo:hi].reshape(512, hi - lo), preferred_element_type=f32)
        u = u * (2.0 / 2048.0)
        if q >= TWO:
            up_all[x, :, lo - SPLIT : hi - SPLIT] = u.astype(bf16)
            ref = up_all.at[x, :, lo - SPLIT : hi - SPLIT]
            for k in (2, 1, 3):
                xs[k, q] = send(ref, ref, xs_s.at[k - 1, q], xs_r.at[k - 1, q], xid(k))
            return
        u = u.reshape(NX, 16, hi - lo)
        up_acc[:, :, lo:hi] = u
        xs_snd[:, :, lo:hi] = u.astype(bf16)
        for k in (2, 1, 3):
            xs[k, q] = send(
                xs_snd.at[lax.rem(x + k, NX), :, lo:hi], xs_rcv.at[k - 1, :, lo:hi],
                xs_s.at[k - 1, q], xs_r.at[k - 1, q], xid(k),
            )

    def up_sum(q):
        lo, hi = CHUNKS[q]
        total = up_acc[x, :, lo:hi]
        for k in (1, 2, 3):
            xs[k, q].wait_recv()
            total = total + xs_rcv[k - 1, :, lo:hi].astype(f32)
        xg_snd[:, lo:hi] = total.astype(bf16)
        for k in (2, 1, 3):
            xg[k, q] = send(
                xg_snd.at[:, lo:hi], xg_rcv.at[k - 1, :, lo:hi],
                xg_s.at[k - 1, q], xg_r.at[k - 1, q], xid(k),
            )

    ga[0, 4].wait_recv()
    swap = send(GA, GB, ab_s, ab_r, sib)
    last(0)
    group_add(3, 0)
    group_own(2)
    swap.wait_recv()
    for half, src in ((c, GA), (1 - c, GB)):
        v = src[...].astype(f32)
        a_all[:, 2 * half] = v[:, :, :64]
        a_all[:, 2 * half + 1] = v[:, :, 64:]
    at_ref[...] = a_all[...].reshape(512, R).T.astype(bf16)
    up_part(0)
    for q in range(1, Q):
        last(q)
        group_add(3, q)
        if q < Q - 1:
            up_part(q)
    group_pair(3)
    up_part(Q - 1)
    group_own(3)

    for q in range(TWO):
        up_sum(q)
    group_end(0)
    group_end(1)

    group_end(2)
    drain(24)
    group_end(3)
    for i in range(4):
        a = zfin[lax.rem(2 * i - y + NY, NY)]
        b = zfin[lax.rem(2 * i + 1 - y + NY, NY)]
        out_ref[:, i * 128 : i * 128 + 128] = jnp.concatenate([a, b], axis=1).astype(bf16)

    for q in range(TWO, Q):
        for k in (1, 2, 3):
            xs[k, q].wait_recv()
    gu_ref[:, SPLIT:] = (
        up_all[0].astype(f32) + up_all[1].astype(f32) + up_all[2].astype(f32) + up_all[3].astype(f32)
    )
    for q in range(TWO):
        for k in (1, 2, 3):
            xg[k, q].wait_recv()
    gu_ref[pl.ds(pl.multiple_of(x * 16, 16), 16), :SPLIT] = xg_snd[...].astype(f32)
    for k in (1, 2, 3):
        at = pl.multiple_of(lax.rem(x - k + NX, NX) * 16, 16)
        gu_ref[pl.ds(at, 16), :SPLIT] = xg_rcv[k - 1].astype(f32)
    for cp in gds:
        cp.wait_recv()
    gd_ref[...] = gd_all[0] + gd_all[1] + gd_all[2] + gd_all[3]
    drain()


def finish(out_ref, gd_ref, gu_ref, out_hbm, gd_hbm, gu_hbm, sem):
    copies = [
        pltpu.make_async_copy(src, dst, sem.at[i])
        for i, (src, dst) in enumerate(((gu_ref, gu_hbm), (out_ref, out_hbm), (gd_ref, gd_hbm)))
    ]
    for cp in copies:
        cp.start()
    for cp in copies:
        cp.wait()


def group_scratch(n):
    d, t = (PD // 2, 128) if n == 64 else (PD, n)
    return [
        pltpu.VMEM((NZ, d, t), bf16),
        pltpu.VMEM((NZ, d, t), bf16),
        pltpu.VMEM((NZ, d, t), bf16),
        pltpu.VMEM((NZ - 1, d, t), bf16),
        pltpu.VMEM((NZ, PD, n), f32),
        pltpu.VMEM((NZ, PD, n), f32),
    ]


def per_device(tokens, codes, scales, down, up, up_branch, hidden_grad):
    vmem = pl.BlockSpec(memory_space=pltpu.VMEM)
    hbm = pl.BlockSpec(memory_space=pl.ANY)
    dma = pltpu.SemaphoreType.DMA
    scratch = [
        pltpu.VMEM((PD, 512), bf16),
        pltpu.VMEM((D, F), bf16),
        pltpu.VMEM((8, F), bf16),
        pltpu.VMEM((R, D), bf16),
        pltpu.VMEM((R, F), bf16),
        pltpu.VMEM((OWN, F), bf16),
        pltpu.VMEM((OWN, F), bf16),
        pltpu.VMEM((8, F), f32),
        pltpu.VMEM((NZ, 2, PD, F), bf16),
        pltpu.VMEM((NZ, 2, PD, 128), bf16),
        pltpu.VMEM((4, NZ, 2, PD, 128), bf16),
        pltpu.VMEM((2, NZ, 2, PD // 2, 128), bf16),
        pltpu.VMEM((128, D), bf16),
        pltpu.VMEM((NY, OWN, F), f32),
        pltpu.VMEM((NY, OWN, 128), f32),
        pltpu.VMEM((2, 4, OWN, F), bf16),
        pltpu.VMEM((2, 4, OWN, F), bf16),
        pltpu.VMEM((2, 4, 16, 128), bf16),
        pltpu.VMEM((2, 4, 16, 128), bf16),
        pltpu.VMEM((NY, OWN, F), bf16),
        pltpu.VMEM((NY, 16, 128), bf16),
        pltpu.VMEM((NY, 16, 128), bf16),
        pltpu.VMEM((NY, 4, 16, R), f32),
        pltpu.VMEM((4, 4, 128), f32),
        pltpu.VMEM((R, OWN), f32),
        pltpu.VMEM((R, OWN), f32),
        pltpu.VMEM((NZ, 8, OWN), f32),
        pltpu.VMEM((NZ - 1, 8, OWN), f32),
        pltpu.VMEM((4, OWN), f32),
        pltpu.VMEM((NY - 1, 4, OWN), f32),
        pltpu.VMEM((NY, PD, OWN), f32),
        pltpu.VMEM((R, 512), bf16),
        pltpu.VMEM((NX, 16, SPLIT), f32),
        pltpu.VMEM((NX, R, F - SPLIT), bf16),
        pltpu.VMEM((NX, 16, SPLIT), bf16),
        pltpu.VMEM((NX - 1, 16, SPLIT), bf16),
        pltpu.VMEM((16, SPLIT), bf16),
        pltpu.VMEM((NX - 1, 16, SPLIT), bf16),
        pltpu.VMEM((NX, 4, D), f32),
    ]
    for g in GROUPS:
        scratch += group_scratch(64 * len(g))
    scratch += [
        dma((7,)),
        dma((5, 7)), dma((5, 7)),
        dma((5,)), dma((5,)),
        dma((2, 4, Q)), dma((2, 4, Q)),
        dma((2, 4, Q)), dma((2, 4, Q)),
        dma((2, 4)), dma((2, 4)),
        dma((2, 4)), dma((2, 4)),
        dma, dma,
        dma((4,)), dma((4,)),
        dma((4, 7)), dma((4, 7)),
        dma, dma,
        dma((7,)), dma((7,)),
        dma((7,)), dma((7,)),
        dma((3, Q)), dma((3, Q)),
        dma((3, Q)), dma((3, Q)),
        dma((3,)), dma((3,)),
    ]
    shapes = (((PD, 512), bf16), ((4, D), f32), ((R, F), f32))
    parts = pl.pallas_call(
        kernel,
        out_shape=tuple(pltpu.VMEM(*s) for s in shapes),
        in_specs=[hbm] * 7,
        out_specs=(vmem,) * 3,
        scratch_shapes=scratch,
        compiler_params=pltpu.CompilerParams(
            collective_id=0, has_side_effects=True, vmem_limit_bytes=56 << 20
        ),
    )(tokens.T, codes, scales, down.T, up, up_branch, hidden_grad)
    out_t, gd_t, gu = pl.pallas_call(
        finish,
        out_shape=tuple(jax.ShapeDtypeStruct(*s) for s in shapes),
        in_specs=[hbm] * 3,
        out_specs=(hbm,) * 3,
        scratch_shapes=[dma((3,))],
    )(*(pltpu.with_memory_space_constraint(a, pltpu.VMEM) for a in parts))
    return out_t.T, gd_t.T, gu


def solution(mesh):
    return jax.shard_map(
        per_device,
        mesh=mesh,
        in_specs=(
            P("dp", ("row", "col")),
            P("row", "col"),
            P("row", "col"),
            P("row", None),
            P(None, "col"),
            P(("dp", "row"), "col"),
            P(("dp", "row"), "col"),
        ),
        out_specs=(P("dp", ("row", "col")), P("row", "col"), P(None, "col")),
        check_vma=False,
    )
```
